256 devices in a mesh: branch: 2 (over x_hi), row: 16 (over z, x_lo), col: 8 (over y, core).
Axes of the slice: x: 4 (x_hi: 2, x_lo: 2; x = x_hi * 2 + x_lo), y: 4, z: 8, core: 2. Of those that a mesh axis runs over, the one named last changes fastest.
Arguments:
- queries: bfloat16 [2, 12288, 2048], P('branch', ('row', 'col')), may hold values from -6 to 6
- keys: bfloat16 [2, 12288, 2048], P('branch', ('row', 'col')), may hold values from -6 to 6
- values: bfloat16 [2, 12288, 2048], P('branch', ('row', 'col')), may hold values from -6 to 6
- text_keys: bfloat16 [2, 256, 2048], P('branch'), may hold values from -8 to 8
- text_values: bfloat16 [2, 256, 2048], P('branch'), may hold values from -6 to 6
- text_lengths: int32 [2], P('branch'), may hold values from 1 to 256, as said below
- step_index: int32 [1], replicated, may hold values from 40 to 49
- out_proj: bfloat16 [2048, 64], replicated, may hold values from -0.125 to 0.125
- latent: float32 [6, 128, 64, 16], P(None, 'row', 'col'), may hold values from -6 to 6
- conv_in_w: bfloat16 [3, 3, 3, 16, 512], replicated, may hold values from -0.3125 to 0.3125
- conv_in_b: float32 [512], replicated, may hold values from -1.5 to 1.5
- conv_mid_w: bfloat16 [3, 3, 3, 512, 512], P(None, None, None, None, 'branch'), may hold values from -0.0546875 to 0.0546875
- conv_mid_b: float32 [512], P('branch'), may hold values from -1.5 to 1.5
Outputs:
- guided: float32 [6, 128, 64, 16], P(None, 'row', 'col')
- decoded: float32 [6, 128, 64, 512], P(None, 'row', 'col', 'branch')
The draws below stay inside these ranges and needn't reach their ends.
Inputs may be any that keep to these rules, and one draw needn't show every extreme that they name: `text_lengths`: one of the two branches has the full 256 text tokens.
All inputs are finite; a program needn't handle non-finite values.
Results may differ from the reference program's by a relative error of at most 0.0054.
Values may be sent and summed in bfloat16 or wider, within the bound.
A program may use at most 128 MiB of HBM per device.

```python
import jax
import jax.numpy as jnp
from jax import lax

FRAMES = 6
TROWS = 4
TCOLS = 4
HEADS = 16
HD = 128
TXT = 256
LAT_CH = 16
VAE_CH = 512
BRANCHES = 2
TOKENS = 12288
PATCH_OUT = 64
HP = 128
WP = 64
N_ROW = 16
N_COL = 8


def draw_queries(key, part):
    base = 1.5 * jax.random.normal(jax.random.fold_in(key, 1), (BRANCHES, TOKENS, HEADS * HD), jnp.float32)
    base = jnp.clip(base, -6.0, 6.0)
    return base.astype(jnp.bfloat16)


def draw_keys(key, part):
    base = 1.5 * jax.random.normal(jax.random.fold_in(key, 2), (BRANCHES, TOKENS, HEADS * HD), jnp.float32)
    base = jnp.clip(base, -6.0, 6.0)
    return base.astype(jnp.bfloat16)


def draw_text_lengths(key, part):
    which = jax.random.randint(jax.random.fold_in(key, 3), (), 0, 2)
    other = jax.random.randint(jax.random.fold_in(key, 4), (), 1, TXT + 1)
    return jnp.where(jnp.arange(2) == which, TXT, other).astype(jnp.int32)


def steps_of(key, extent, shards, low, top_value):
    loudness, own = 1.0, jax.random.fold_in(key, 6)
    for dim, parts in shards:
        steps = jnp.exp(jax.random.uniform(jax.random.fold_in(own, dim), (parts,), jnp.float32, low / len(shards), top_value / len(shards)))
        loudness = loudness * jnp.repeat(steps, extent[dim] // parts).reshape([-1 if axis == dim else 1 for axis in range(len(extent))])
    return loudness


def noise(stream_key, dims, width, limit, shards=(), dtype=jnp.bfloat16):
    factor_of = steps_of(stream_key, dims, shards, -0.22, 0.18) if shards else 1.0
    drawn = jax.random.normal(stream_key, dims, jnp.float32) * width * factor_of
    return jnp.minimum(jnp.maximum(drawn, -limit), limit).astype(dtype)


def setup_inputs(seed: int = 0) -> dict:
    splits = jax.random.split(jax.random.key(seed), 14)
    return {
        "queries": draw_queries(jax.random.fold_in(splits[13], 71), 0),
        "keys": draw_keys(jax.random.fold_in(splits[13], 71), 0),
        "values": noise(splits[2], (BRANCHES, TOKENS, HEADS * HD), 1.0, 6.0, ((0, 2), (1, 128))),
        "text_keys": noise(splits[3], (BRANCHES, TXT, HEADS * HD), 2.0, 8.0, ((0, 2),)),
        "text_values": noise(splits[4], (BRANCHES, TXT, HEADS * HD), 1.0, 6.0, ((0, 2),)),
        "text_lengths": draw_text_lengths(jax.random.fold_in(splits[13], 71), 0),
        "step_index": jax.random.randint(splits[6], (1,), 40, 50).astype(jnp.int32),
        "out_proj": noise(splits[7], (HEADS * HD, PATCH_OUT), (HEADS * HD) ** -0.5, 0.125),
        "latent": noise(splits[8], (FRAMES, HP, WP, LAT_CH), 1.0, 6.0, ((1, 16), (2, 8)), jnp.float32),
        "conv_in_w": noise(splits[9], (3, 3, 3, LAT_CH, VAE_CH), (27 * LAT_CH) ** -0.5, 0.3125),
        "conv_in_b": noise(splits[10], (VAE_CH,), 0.3, 1.5, (), jnp.float32),
        "conv_mid_w": noise(splits[11], (3, 3, 3, VAE_CH, VAE_CH), (27 * VAE_CH) ** -0.5, 0.0546875, ((4, 2),)),
        "conv_mid_b": noise(splits[12], (VAE_CH,), 0.3, 1.5, ((0, 2),), jnp.float32),
    }


def sigma_at(index):
    s = 1.0 - index.astype(jnp.float32) / 50.0
    return 7.0 * s / (1.0 + 6.0 * s)


def attend(queries_b, keys_b, values_b, text_k, text_v, text_count):
    all_keys = jnp.concatenate([keys_b, text_k], 0).astype(jnp.float32)
    all_values = jnp.concatenate([values_b, text_v], 0).astype(jnp.float32)
    usable = jnp.concatenate([jnp.ones((TOKENS,), bool), jnp.arange(TXT) < text_count])
    query_rows = 256 if TOKENS % 256 == 0 else TOKENS
    blocks = queries_b.reshape(TOKENS // query_rows, query_rows, HEADS, HD)

    def one_block(block):
        scores = jnp.einsum("qhe,khe->qhk", block.astype(jnp.float32), all_keys) * (HD ** -0.5)
        scores = jnp.where(usable[None, None, :], scores, -1.0e30)
        row_max = jnp.max(scores, axis=2, keepdims=True)
        expo = jnp.where(usable[None, None, :], jnp.exp(scores - row_max), 0.0)
        denom = jnp.sum(expo, axis=2)
        weights = lax.optimization_barrier(expo.astype(jnp.bfloat16)).astype(jnp.float32)
        weighted = jnp.einsum("qhk,khe->qhe", weights, all_values)
        return (weighted / denom[..., None]).astype(jnp.bfloat16)

    return lax.map(one_block, blocks).reshape(TOKENS, HEADS * HD)


def unpatchify(tokens):
    grid = tokens.reshape(N_ROW, N_COL, FRAMES, TROWS, TCOLS, 2, 2, LAT_CH)
    grid = grid.transpose(2, 0, 3, 5, 1, 4, 6, 7)
    return grid.reshape(FRAMES, HP, WP, LAT_CH)


def causal_conv(field, weight):
    frame_count, row_count, col_count = field.shape[0], field.shape[1], field.shape[2]
    padded = jnp.pad(field, ((0, 0), (1, 1), (1, 1), (0, 0)))
    padded = jnp.concatenate([padded[:1], padded[:1], padded], 0)
    result = jnp.zeros((frame_count, row_count, col_count, weight.shape[4]), jnp.float32)
    for tap_t in range(3):
        for tap_h in range(3):
            for tap_w in range(3):
                window = padded[tap_t:tap_t + frame_count, tap_h:tap_h + row_count, tap_w:tap_w + col_count]
                result = result + jnp.einsum("fhwc,co->fhwo", window.astype(jnp.float32), weight[tap_t, tap_h, tap_w].astype(jnp.float32))
    return result


def reference(queries, keys, values, text_keys, text_values, text_lengths, step_index, out_proj, latent, conv_in_w, conv_in_b, conv_mid_w, conv_mid_b):
    velocities = []
    for which in range(2):
        attn = attend(queries[which].reshape(TOKENS, HEADS, HD), keys[which].reshape(TOKENS, HEADS, HD), values[which].reshape(TOKENS, HEADS, HD), text_keys[which].reshape(TXT, HEADS, HD), text_values[which].reshape(TXT, HEADS, HD), text_lengths[which])
        velocities.append(jnp.dot(attn, out_proj, preferred_element_type=jnp.float32))
    guided_tokens = velocities[1] + 6.0 * (velocities[0] - velocities[1])
    guided = unpatchify(guided_tokens)
    index = step_index[0]
    advance = sigma_at(index + 1) - sigma_at(index)
    moved = (latent + advance * guided).astype(jnp.bfloat16)
    hidden = causal_conv(moved, conv_in_w) + conv_in_b.astype(jnp.float32)
    act = jax.nn.silu(hidden).astype(jnp.bfloat16)
    decoded = hidden + causal_conv(act, conv_mid_w) + conv_mid_b.astype(jnp.float32)
    return (guided, decoded)
```

```python
import functools

import jax
import jax.numpy as jnp
import numpy as np
from jax import lax
from jax.experimental import pallas as pl
from jax.experimental.pallas import tpu as pltpu
from jax.sharding import PartitionSpec as P

HD = 128
MESH = pl.DeviceIdType.MESH
NEG_FILL = -1e30
COND_GAIN = 6.0
UNCOND_GAIN = -5.0
SCORE_GAIN = float(HD**-0.5 * np.log2(np.e))

Z_ORDER = (0, 1, 7, 2, 6, 3, 5, 4)
Z_COUNT = 8
SLOTS = 16
TOK = 96
HALF = 48
KV_ROWS = TOK + HALF
GROUPS = 4
PER_GROUP = 4
QUERIES = SLOTS * TOK
CHUNK = 4 * PER_GROUP * TOK
Q_TILE = 512

BF16 = jnp.bfloat16
F32 = jnp.float32


def row_partner(row, slot, sign):
    z, x = row // 2, row % 2
    dz = Z_ORDER[slot // 2]
    dz = dz if sign > 0 else (Z_COUNT - dz) % Z_COUNT
    return lax.rem(z + dz, Z_COUNT) * 2 + lax.rem(x + slot % 2, 2)


def attend(q_ref, o_ref, m_ref, key_ref, value_ref, key_count, usable):
    @pl.loop(0, QUERIES // Q_TILE)
    def _(tile):
        rows = pl.ds(pl.multiple_of(tile * Q_TILE, Q_TILE), Q_TILE)
        scores = lax.dot_general(
            q_ref[rows, :],
            key_ref[0:key_count, :],
            (((1,), (1,)), ((), ())),
            preferred_element_type=F32,
        )
        if usable is not None:
            scores = jnp.where(usable, scores, NEG_FILL)
        before = m_ref[rows, 0:1]
        top = jnp.maximum(before, jnp.max(scores, axis=1, keepdims=True) * SCORE_GAIN)
        weights = jnp.exp2(scores * SCORE_GAIN - top).astype(BF16)
        o_ref[rows, :] = o_ref[rows, :] * jnp.exp2(before - top) + jnp.dot(
            weights, value_ref[0:key_count, :], preferred_element_type=F32
        )
        m_ref[rows, :] = jnp.broadcast_to(top, (Q_TILE, 128))


def attention_kernel(
    q_in, k_in, v_in, w_ref, tk_hbm, tv_hbm, len_ref,
    vel_ref,
    kv_out, q_out, kv, q_ref, o_ref, m_ref, key_ref, value_ref, tk_ref, tv_ref, sh_out, sh_in,
    kv_send, kv_recv, q_send, q_recv, hop_send, hop_recv, sh_send, sh_recv, text_sem,
):
    row, col = lax.axis_index("row"), lax.axis_index("col")
    y, core = col // 2, col % 2
    up = lax.rem(y + 1, 4) * 2 + core
    down = lax.rem(y + 3, 4) * 2 + core
    onward = lax.rem(y + 1 + 2 * core, 4) * 2 + core
    sibling = y * 2 + 1 - core

    barrier = pltpu.get_barrier_semaphore()
    for slot in range(1, SLOTS):
        pl.semaphore_signal(
            barrier, inc=1, device_id={"row": row_partner(row, slot, 1)}, device_id_type=MESH
        )
    for other in (up, down, sibling):
        pl.semaphore_signal(barrier, inc=1, device_id={"col": other}, device_id_type=MESH)

    head_cols = pl.ds(pl.multiple_of(row * HD, HD), HD)
    text_copies = [
        pltpu.make_async_copy(tk_hbm.at[0, :, head_cols], tk_ref, text_sem.at[0]),
        pltpu.make_async_copy(tv_hbm.at[0, :, head_cols], tv_ref, text_sem.at[1]),
    ]
    for copy in text_copies:
        copy.start()

    for head in range(SLOTS):
        cols = slice(head * HD, (head + 1) * HD)
        kv_out[head, 0:TOK, :] = k_in[0, :, cols]
        projected = jnp.dot(v_in[0, :, cols], w_ref[cols, :], preferred_element_type=F32)
        kv_out[head, TOK:KV_ROWS, :] = jnp.concatenate(
            [projected[0:HALF], projected[HALF:TOK]], axis=1
        ).astype(BF16)
        q_out[head] = q_in[0, :, cols]

    def kv_copy(slot):
        there = row_partner(row, slot, 1)
        return pltpu.make_async_remote_copy(
            src_ref=kv_out.at[there],
            dst_ref=kv.at[0, slot],
            send_sem=kv_send.at[slot],
            recv_sem=kv_recv.at[slot],
            device_id={"row": there},
            device_id_type=MESH,
        )

    def q_copy(slot):
        there = row_partner(row, slot, 1)
        return pltpu.make_async_remote_copy(
            src_ref=q_out.at[there],
            dst_ref=q_ref.at[pl.ds(slot * TOK, TOK)],
            send_sem=q_send.at[slot],
            recv_sem=q_recv.at[slot],
            device_id={"row": there},
            device_id_type=MESH,
        )

    def hop_copy(kind, group):
        src, dst, there = (
            (0, 1, up),
            (0, 2, down),
            (1 + core, 3, onward),
            (0, 4, sibling),
            (1, 5, sibling),
            (2, 6, sibling),
            (3, 7, sibling),
        )[kind]
        part = pl.ds(group * PER_GROUP, PER_GROUP)
        return pltpu.make_async_remote_copy(
            src_ref=kv.at[src, part],
            dst_ref=kv.at[dst, part],
            send_sem=hop_send.at[kind, group],
            recv_sem=hop_recv.at[kind, group],
            device_id={"col": there},
            device_id_type=MESH,
        )

    def share_copy(slot):
        return pltpu.make_async_remote_copy(
            src_ref=sh_out.at[slot],
            dst_ref=sh_in.at[slot],
            send_sem=sh_send.at[slot],
            recv_sem=sh_recv.at[slot],
            device_id={"row": row_partner(row, slot, -1)},
            device_id_type=MESH,
        )

    pl.semaphore_wait(barrier, SLOTS - 1 + 3)
    for slot in range(1, PER_GROUP):
        kv_copy(slot).start()
    for slot in range(1, SLOTS):
        q_copy(slot).start()
    for slot in range(PER_GROUP, SLOTS):
        kv_copy(slot).start()

    kv[0, 0] = kv_out[row]
    q_ref[0:TOK, :] = q_out[row]
    o_ref[...] = jnp.zeros_like(o_ref)
    m_ref[...] = jnp.full_like(m_ref, NEG_FILL)

    lane = lax.broadcasted_iota(jnp.int32, (HALF, HD), 1)
    ones = jnp.where(lane == HD // 2, 1.0, 0.0).astype(F32)

    def first_hop(group):
        for slot in range(group * PER_GROUP, (group + 1) * PER_GROUP):
            if slot:
                kv_copy(slot).wait_recv()
        for kind in (0, 1, 3):
            hop_copy(kind, group).start()

    def second_hop(group):
        hop_copy(0, group).wait_recv()
        hop_copy(1, group).wait_recv()
        for kind in (2, 4, 5):
            hop_copy(kind, group).start()

    def third_hop(group):
        hop_copy(2, group).wait_recv()
        hop_copy(6, group).start()

    def from_sibling(group):
        for kind in (3, 4, 5, 6):
            hop_copy(kind, group).wait_recv()

    first_hop(0)

    for copy in text_copies:
        copy.wait()
    text_rows = tk_ref.shape[0]
    own_proj = w_ref[pl.ds(pl.multiple_of(row * HD, HD), HD), :]
    text_projected = jnp.dot(tv_ref[...], own_proj, preferred_element_type=F32)
    text_lane = lax.broadcasted_iota(jnp.int32, (text_rows, HD // 2), 1)
    value_ref[0:text_rows, :] = jnp.concatenate(
        [text_projected, jnp.where(text_lane == 0, 1.0, 0.0).astype(F32)], axis=1
    ).astype(BF16)
    for slot in range(1, SLOTS):
        q_copy(slot).wait_recv()
    usable = lax.broadcasted_iota(jnp.int32, (Q_TILE, text_rows), 1) < len_ref[0]
    attend(q_ref, o_ref, m_ref, tk_ref, value_ref, text_rows, usable)

    second_hop(0)
    first_hop(1)
    third_hop(0)

    def before_chunk_1():
        second_hop(1)
        first_hop(2)
        from_sibling(0)

    def before_chunk_2():
        third_hop(1)
        second_hop(2)
        first_hop(3)

    def before_chunk_3():
        third_hop(2)
        second_hop(3)
        from_sibling(1)

    def before_chunk_4():
        third_hop(3)

    def before_chunk_5():
        from_sibling(2)

    def before_chunk_7():
        from_sibling(3)

    steps = {
        1: before_chunk_1,
        2: before_chunk_2,
        3: before_chunk_3,
        4: before_chunk_4,
        5: before_chunk_5,
        7: before_chunk_7,
    }

    @pl.loop(0, 2 * GROUPS)
    def _(chunk):
        for when, step in steps.items():
            pl.when(chunk == when)(step)
        group, side = chunk // 2, chunk % 2

        for part in range(4):
            for slot in range(PER_GROUP):
                at = (part * PER_GROUP + slot) * TOK
                block = kv.at[4 * side + part, group * PER_GROUP + slot]
                key_ref[at : at + TOK, :] = block[0:TOK, :]
                packed = block[TOK:KV_ROWS, :].astype(F32)
                value_ref[at : at + HALF, :] = jnp.where(lane < HD // 2, packed, ones).astype(BF16)
                value_ref[at + HALF : at + TOK, :] = jnp.where(
                    lane < HD // 2, pltpu.roll(packed, HD // 2, 1), ones
                ).astype(BF16)
        attend(q_ref, o_ref, m_ref, key_ref, value_ref, CHUNK, None)

    total = None
    for slot in range(SLOTS):
        out = o_ref[slot * TOK : (slot + 1) * TOK, :]
        share = out[:, 0 : HD // 2] / out[:, HD // 2 : HD // 2 + 1]
        packed = jnp.concatenate([share[0:HALF], share[HALF:TOK]], axis=1)
        if slot == 0:
            total = packed
        else:
            sh_out[slot] = packed.astype(BF16)
            share_copy(slot).start()
    for slot in range(1, SLOTS):
        share_copy(slot).wait_recv()
        total = total + sh_in[slot].astype(F32)
    vel_ref[...] = total

    for slot in range(1, SLOTS):
        kv_copy(slot).wait_send()
        q_copy(slot).wait_send()
        share_copy(slot).wait_send()
    for group in range(GROUPS):
        for kind in range(7):
            hop_copy(kind, group).wait_send()


def tile_velocity(queries, keys, values, out_proj, text_keys, text_values, text_lengths):
    text_rows = text_keys.shape[1]
    vmem = pl.BlockSpec(memory_space=pltpu.VMEM)
    dma = pltpu.SemaphoreType.DMA
    return pl.pallas_call(
        attention_kernel,
        out_shape=jax.ShapeDtypeStruct((HALF, HD), F32),
        in_specs=[
            vmem, vmem, vmem, vmem,
            pl.BlockSpec(memory_space=pl.ANY),
            pl.BlockSpec(memory_space=pl.ANY),
            pl.BlockSpec(memory_space=pltpu.SMEM),
        ],
        out_specs=vmem,
        scratch_shapes=[
            pltpu.VMEM((SLOTS, KV_ROWS, HD), BF16),
            pltpu.VMEM((SLOTS, TOK, HD), BF16),
            pltpu.VMEM((8, SLOTS, KV_ROWS, HD), BF16),
            pltpu.VMEM((QUERIES, HD), BF16),
            pltpu.VMEM((QUERIES, HD), F32),
            pltpu.VMEM((QUERIES, HD), F32),
            pltpu.VMEM((CHUNK, HD), BF16),
            pltpu.VMEM((CHUNK, HD), BF16),
            pltpu.VMEM((text_rows, HD), BF16),
            pltpu.VMEM((text_rows, HD), BF16),
            pltpu.VMEM((SLOTS, HALF, HD), BF16),
            pltpu.VMEM((SLOTS, HALF, HD), BF16),
            dma((SLOTS,)), dma((SLOTS,)), dma((SLOTS,)), dma((SLOTS,)),
            dma((7, GROUPS)), dma((7, GROUPS)), dma((SLOTS,)), dma((SLOTS,)), dma((2,)),
        ],
        compiler_params=pltpu.CompilerParams(
            collective_id=0, has_side_effects=True, vmem_limit_bytes=50 * 2**20
        ),
        name="attention",
    )(queries, keys, values, out_proj, text_keys, text_values, text_lengths)


AROUND = tuple((dr, dc) for dr in (-1, 0, 1) for dc in (-1, 0, 1))
FRAMES, TROWS, TCOLS = 6, 4, 4
PLACES = TROWS * TCOLS
ROWS = FRAMES * PLACES
PADDED_ROWS = (FRAMES + 2) * PLACES


def pick_matrix():
    pick = np.zeros((3, 3, FRAMES // 2, TROWS, TCOLS, 9, FRAMES // 2, TROWS, TCOLS), np.float32)
    for e, g, f, i, j in np.ndindex(3, 3, FRAMES // 2, TROWS, TCOLS):
        r, c = i + e - 1, j + g - 1
        tile = AROUND.index((r // TROWS, c // TCOLS))
        pick[e, g, f, i, j, tile, f, r % TROWS, c % TCOLS] = 1.0
    return pick.reshape(9 * HALF, 9 * HALF)


def sigma_at(index):
    s = 1.0 - index / 50.0
    return 7.0 * s / (1.0 + 6.0 * s)


def decoder_kernel(
    row_count, col_count,
    vel_ref, lat_ref, pick_ref, step_ref, win_ref, bin_ref, wmid_hbm, bmid_ref,
    guided_ref, out_ref,
    mine, raw, raw_in, near, moved, shifted, w_in, wmid, act, center,
    send, recv, w_sem,
):
    branch, row, col = lax.axis_index("branch"), lax.axis_index("row"), lax.axis_index("col")

    def place(side, tile):
        dr, dc = AROUND[tile]
        return {
            "branch": lax.rem(branch + side, 2),
            "row": lax.rem(row + dr + row_count, row_count),
            "col": lax.rem(col + dc + col_count, col_count),
        }

    peers = [(side, tile) for side in (0, 1) for tile in range(9) if (side, tile) != (0, 4)]

    barrier = pltpu.get_barrier_semaphore()
    for side, tile in peers:
        pl.semaphore_signal(barrier, inc=1, device_id=place(side, tile), device_id_type=MESH)

    w_copies = []
    for b in range(3):
        for c in range(3):
            for a in range(3):
                at = (b * 3 + c) * 3 + a
                w_copies.append(
                    pltpu.make_async_copy(
                        wmid_hbm.at[a, b, c],
                        wmid.at[b * 3 + c, pl.ds(a * 512, 512)],
                        w_sem.at[at],
                    )
                )
    for copy in w_copies:
        copy.start()

    index = step_ref[0].astype(F32)
    advance = sigma_at(index + 1.0) - sigma_at(index)
    first = branch == 0
    velocity = vel_ref[...]
    raw[...] = velocity
    keep = jnp.where(first, 1.0, 0.0)
    gain = jnp.where(first, COND_GAIN, UNCOND_GAIN) * advance
    mine[...] = lat_ref[...] * keep + velocity * gain

    def copy_to(side, tile):
        if tile == 4:
            src, dst = raw, raw_in
        else:
            src, dst = mine, near.at[side, 8 - tile]
        return pltpu.make_async_remote_copy(
            src_ref=src,
            dst_ref=dst,
            send_sem=send.at[side, tile],
            recv_sem=recv.at[side, tile],
            device_id=place(side, tile),
            device_id_type=MESH,
        )

    pl.semaphore_wait(barrier, len(peers))
    for side, tile in peers:
        copy_to(side, tile).start()

    zero = jnp.zeros((16, 512), BF16)
    for a in range(3):
        for r in range(4):
            for c in range(4):
                lanes = (((r // 2) * 2 + c // 2) * 4 + (r % 2) * 2 + c % 2) * 16
                for pp in range(2):
                    for ss in range(2):
                        inside = 0 <= r - pp < 3 and 0 <= c - ss < 3
                        w_in[
                            a * 256 + lanes : a * 256 + lanes + 16,
                            (pp * 2 + ss) * 512 : (pp * 2 + ss + 1) * 512,
                        ] = win_ref[a, r - pp, c - ss] if inside else zero

    for side, tile in peers:
        copy_to(side, tile).wait_recv()

    cond = jnp.where(first, raw[...], raw_in[...])
    uncond = jnp.where(first, raw_in[...], raw[...])
    guided = COND_GAIN * cond + UNCOND_GAIN * uncond
    guided_ref[...] = guided
    for tile, (dr, dc) in enumerate(AROUND):
        if tile == 4:
            value = lat_ref[...] + advance * guided
        else:
            there_row, there_col = row + dr, col + dc
            there = (
                (there_row >= 0)
                & (there_row < row_count)
                & (there_col >= 0)
                & (there_col < col_count)
            )
            value = (near[0, tile] + near[1, tile]) * jnp.where(there, 1.0, 0.0)
        moved[tile * HALF : (tile + 1) * HALF, :] = value.astype(BF16)

    picked = jnp.dot(pick_ref[...], moved[...], preferred_element_type=F32)
    lane = lax.broadcasted_iota(jnp.int32, (HALF, HD), 1)
    low = lane < HD // 2
    for e in range(3):
        for g in range(2):
            at = (e * 3 + g) * HALF
            here, right = picked[at : at + HALF], picked[at + HALF : at + 2 * HALF]
            early = jnp.where(low, here, pltpu.roll(right, HD // 2, 1)).astype(BF16)
            late = jnp.where(low, pltpu.roll(here, HD // 2, 1), right).astype(BF16)
            shifted[e, g, 0:PLACES, :] = early[0:PLACES]
            shifted[e, g, PLACES : 2 * PLACES, :] = early[0:PLACES]
            shifted[e, g, 2 * PLACES : 2 * PLACES + HALF, :] = early
            shifted[e, g, 2 * PLACES + HALF : PADDED_ROWS, :] = late

    patches = jnp.concatenate(
        [
            jnp.concatenate(
                [
                    shifted[db + du, dc, a * PLACES : a * PLACES + ROWS, :]
                    for a in range(3)
                    for du in range(2)
                ],
                axis=1,
            )
            for db in range(2)
            for dc in range(2)
        ],
        axis=0,
    )

    at = lax.broadcasted_iota(jnp.int32, (ROWS, 1), 0)
    row_at, col_at = (at // TCOLS) % TROWS, at % TCOLS
    bias_in = bin_ref[...]
    for pp in range(2):
        for ss in range(2):
            kind = pp * 2 + ss
            for half in range(2):
                cols = slice(half * 256, (half + 1) * 256)
                hidden = (
                    jnp.dot(
                        patches,
                        w_in[:, kind * 512 + half * 256 : kind * 512 + (half + 1) * 256],
                        preferred_element_type=F32,
                    )
                    + bias_in[:, cols]
                )
                for db in range(2):
                    for dc in range(2):
                        shift = db * 2 + dc
                        block = hidden[shift * ROWS : (shift + 1) * ROWS]
                        if (db, dc) == (1 - pp, 1 - ss):
                            center[kind, :, cols] = block
                        y_at = row * (2 * TROWS) - 1 + 2 * (row_at + db) + pp
                        x_at = col * (2 * TCOLS) - 1 + 2 * (col_at + dc) + ss
                        inside = (
                            (y_at >= 0)
                            & (y_at < row_count * 2 * TROWS)
                            & (x_at >= 0)
                            & (x_at < col_count * 2 * TCOLS)
                        )
                        value = jnp.where(inside, block * jax.nn.sigmoid(block), 0.0).astype(BF16)
                        act[kind, shift, 0:PLACES, cols] = value[0:PLACES]
                        act[kind, shift, PLACES : 2 * PLACES, cols] = value[0:PLACES]
                        act[kind, shift, 2 * PLACES : PADDED_ROWS, cols] = value

    total = None
    for b in range(3):
        for c in range(3):
            for a in range(3):
                w_copies[(b * 3 + c) * 3 + a].wait()
            window = []
            for pi in range(2):
                for si in range(2):
                    kind = ((pi + b) % 2) * 2 + (si + c) % 2
                    shift = ((pi + b) // 2) * 2 + (si + c) // 2
                    window.append(
                        jnp.concatenate(
                            [
                                act[kind, shift, a * PLACES : a * PLACES + ROWS, :]
                                for a in range(3)
                            ],
                            axis=1,
                        )
                    )
            term = jnp.dot(
                jnp.concatenate(window, axis=0), wmid[b * 3 + c], preferred_element_type=F32
            )
            total = term if total is None else total + term
    own = pl.ds(pl.multiple_of(branch * 256, 256), 256)
    for pi in range(2):
        for si in range(2):
            phase = pi * 2 + si
            out_ref[phase] = (
                center[(1 - pi) * 2 + (1 - si), :, own]
                + total[phase * ROWS : (phase + 1) * ROWS]
                + bmid_ref[...]
            )

    for side, tile in peers:
        copy_to(side, tile).wait_send()


def decode(velocity, latent_tile, step_index, w_in, b_in, w_mid, b_mid, row_count, col_count):
    vmem = pl.BlockSpec(memory_space=pltpu.VMEM)
    dma = pltpu.SemaphoreType.DMA
    return pl.pallas_call(
        functools.partial(decoder_kernel, row_count, col_count),
        out_shape=(
            jax.ShapeDtypeStruct((HALF, HD), F32),
            jax.ShapeDtypeStruct((4, ROWS, 256), F32),
        ),
        in_specs=[
            vmem, vmem, vmem,
            pl.BlockSpec(memory_space=pltpu.SMEM),
            vmem, vmem,
            pl.BlockSpec(memory_space=pl.ANY),
            vmem,
        ],
        out_specs=(vmem, vmem),
        scratch_shapes=[
            pltpu.VMEM((HALF, HD), F32),
            pltpu.VMEM((HALF, HD), F32),
            pltpu.VMEM((HALF, HD), F32),
            pltpu.VMEM((2, 9, HALF, HD), F32),
            pltpu.VMEM((9 * HALF, HD), BF16),
            pltpu.VMEM((3, 2, PADDED_ROWS, HD), BF16),
            pltpu.VMEM((768, 2048), BF16),
            pltpu.VMEM((9, 1536, 256), BF16),
            pltpu.VMEM((4, 4, PADDED_ROWS, 512), BF16),
            pltpu.VMEM((4, ROWS, 512), F32),
            dma((2, 9)), dma((2, 9)), dma((27,)),
        ],
        compiler_params=pltpu.CompilerParams(
            collective_id=1, has_side_effects=True, vmem_limit_bytes=50 * 2**20
        ),
        name="decoder",
    )(
        velocity, latent_tile, jnp.asarray(pick_matrix(), BF16), step_index,
        w_in, b_in[None, :], w_mid, b_mid[None, :],
    )


def local(
    row_count,
    col_count,
    queries,
    keys,
    values,
    text_keys,
    text_values,
    text_lengths,
    step_index,
    out_proj,
    latent,
    conv_in_w,
    conv_in_b,
    conv_mid_w,
    conv_mid_b,
):
    latent_tile = (
        latent.reshape(2, 3, TROWS, 2, TCOLS, 2, 16)
        .transpose(1, 2, 4, 0, 3, 5, 6)
        .reshape(HALF, HD)
    )
    velocity = tile_velocity(queries, keys, values, out_proj, text_keys, text_values, text_lengths)
    guided, decoded = decode(
        velocity, latent_tile, step_index, conv_in_w, conv_in_b, conv_mid_w, conv_mid_b,
        row_count, col_count,
    )
    guided = (
        guided.reshape(3, TROWS, TCOLS, 2, 2, 2, 16)
        .transpose(3, 0, 1, 4, 2, 5, 6)
        .reshape(latent.shape)
    )
    decoded = (
        decoded.reshape(2, 2, FRAMES, TROWS, TCOLS, 256)
        .transpose(2, 3, 0, 4, 1, 5)
        .reshape(FRAMES, 2 * TROWS, 2 * TCOLS, 256)
    )
    return guided, decoded


def solution(mesh):
    return jax.shard_map(
        functools.partial(local, mesh.shape["row"], mesh.shape["col"]),
        mesh=mesh,
        in_specs=(
            P("branch", ("row", "col"), None),
            P("branch", ("row", "col"), None),
            P("branch", ("row", "col"), None),
            P("branch", None, None),
            P("branch", None, None),
            P("branch"),
            P(),
            P(),
            P(None, "row", "col", None),
            P(),
            P(),
            P(None, None, None, None, "branch"),
            P("branch"),
        ),
        out_specs=(P(None, "row", "col", None), P(None, "row", "col", "branch")),
        check_vma=False,
    )
```

```python
import functools

import jax
import jax.numpy as jnp
import numpy as np
from jax import lax
from jax.experimental import pallas as pl
from jax.experimental.pallas import tpu as pltpu
from jax.sharding import PartitionSpec as P

HD = 128
MESH = pl.DeviceIdType.MESH
NEG_FILL = -1e30
COND_GAIN = 6.0
UNCOND_GAIN = -5.0
SCORE_GAIN = float(HD**-0.5 * np.log2(np.e))

Z_ORDER = (0, 1, 7, 2, 6, 3, 5, 4)
Z_COUNT = 8
SLOTS = 16
TOK = 96
HALF = 48
KV_ROWS = TOK + HALF
GROUPS = 4
PER_GROUP = 4
QUERIES = SLOTS * TOK
CHUNK = 4 * PER_GROUP * TOK
PART = QUERIES // 2

BF16 = jnp.bfloat16
F32 = jnp.float32


def row_partner(row, slot, sign):
    z, x = row // 2, row % 2
    dz = Z_ORDER[slot // 2]
    dz = dz if sign > 0 else (Z_COUNT - dz) % Z_COUNT
    return lax.rem(z + dz, Z_COUNT) * 2 + lax.rem(x + slot % 2, 2)


AROUND = tuple((dr, dc) for dr in (-1, 0, 1) for dc in (-1, 0, 1))
FRAMES, TROWS, TCOLS = 6, 4, 4
PLACES = TROWS * TCOLS
ROWS = FRAMES * PLACES
PADDED_ROWS = (FRAMES + 2) * PLACES


def pick_matrix():
    pick = np.zeros((3, 3, FRAMES // 2, TROWS, TCOLS, 9, FRAMES // 2, TROWS, TCOLS), np.float32)
    for e, g, f, i, j in np.ndindex(3, 3, FRAMES // 2, TROWS, TCOLS):
        r, c = i + e - 1, j + g - 1
        tile = AROUND.index((r // TROWS, c // TCOLS))
        pick[e, g, f, i, j, tile, f, r % TROWS, c % TCOLS] = 1.0
    return pick.reshape(9 * HALF, 9 * HALF)


def sigma_at(index):
    s = 1.0 - index / 50.0
    return 7.0 * s / (1.0 + 6.0 * s)


def attend(q_ref, o_ref, m_ref, part, key_ref, value_ref, usable):
    rows = pl.ds(pl.multiple_of(part * PART, PART), PART)
    scores = lax.dot_general(
        q_ref[rows, :], key_ref[...], (((1,), (1,)), ((), ())), preferred_element_type=F32
    )
    if usable is not None:
        scores = jnp.where(usable, scores, NEG_FILL)
    before = m_ref[rows, :]
    top = jnp.maximum(before, jnp.max(scores, axis=1, keepdims=True) * SCORE_GAIN)
    wide = jnp.concatenate([top] * (scores.shape[1] // HD), axis=1)
    weights = jnp.exp2(scores * SCORE_GAIN - wide).astype(BF16)
    o_ref[rows, :] = o_ref[rows, :] * jnp.exp2(before - top) + jnp.dot(
        weights, value_ref[...], preferred_element_type=F32
    )
    m_ref[rows, :] = top


def step_kernel(
    row_count, col_count,
    q_hbm, k_hbm, v_hbm, w_hbm, tk_hbm, tv_hbm, len_ref,
    lat_hbm, pick_hbm, step_ref, win_hbm, bin_hbm, wmid_hbm, bmid_hbm,
    guided_ref, out_ref,
    v_ref, w_ref, v_out, kv, q_ref, o_ref, m_ref, key_ref, value_ref, tk_ref, tv_ref, text_value, sh_out, sh_in,
    lat_in, pieces, lat_ref, pick_ref, win_ref, bin_ref, bmid_ref,
    mine, raw, raw_in, around, moved, shifted, w_in, wmid, act, center, ordered,
    k_send, k_recv, v_send, v_recv, q_send, q_recv, hop_send, hop_recv, sh_send, sh_recv,
    send, recv, w_sem, in_sem,
):
    branch, row, col = lax.axis_index("branch"), lax.axis_index("row"), lax.axis_index("col")
    y, core = col // 2, col % 2
    up = lax.rem(y + 1, 4) * 2 + core
    down = lax.rem(y + 3, 4) * 2 + core
    opposite = lax.rem(y + 2, 4) * 2 + core
    sibling = y * 2 + 1 - core

    def place(side, tile):
        dr, dc = AROUND[tile]
        return {
            "branch": lax.rem(branch + side, 2),
            "row": lax.rem(row + dr + row_count, row_count),
            "col": lax.rem(col + dc + col_count, col_count),
        }

    peers = [(side, tile) for side in (0, 1) for tile in range(9) if (side, tile) != (0, 4)]

    barrier = pltpu.get_barrier_semaphore()
    for slot in range(1, SLOTS):
        pl.semaphore_signal(
            barrier, inc=1, device_id={"row": row_partner(row, slot, 1)}, device_id_type=MESH
        )
    for other in (up, down, opposite, sibling):
        pl.semaphore_signal(barrier, inc=1, device_id={"col": other}, device_id_type=MESH)
    for side, tile in peers:
        pl.semaphore_signal(barrier, inc=1, device_id=place(side, tile), device_id_type=MESH)

    head_cols = pl.ds(pl.multiple_of(row * HD, HD), HD)
    loads = [
        pltpu.make_async_copy(src, dst, in_sem.at[i])
        for i, (src, dst) in enumerate(
            (
                (v_hbm.at[0], v_ref),
                (w_hbm, w_ref),
                (k_hbm.at[0, :, head_cols], kv.at[0, 0, pl.ds(0, TOK)]),
                (q_hbm.at[0, :, head_cols], q_ref.at[pl.ds(0, TOK)]),
                (tk_hbm.at[0, :, head_cols], tk_ref),
                (tv_hbm.at[0, :, head_cols], tv_ref),
                (win_hbm, win_ref),
                (bin_hbm, bin_ref),
                (bmid_hbm, bmid_ref),
                (pick_hbm, pick_ref),
                (lat_hbm, lat_in),
            )
        )
    ]
    for copy in loads:
        copy.start()

    def k_copy(slot):
        there = row_partner(row, slot, 1)
        return pltpu.make_async_remote_copy(
            src_ref=k_hbm.at[0, :, pl.ds(pl.multiple_of(there * HD, HD), HD)],
            dst_ref=kv.at[0, slot, pl.ds(0, TOK)],
            send_sem=k_send.at[slot],
            recv_sem=k_recv.at[slot],
            device_id={"row": there},
            device_id_type=MESH,
        )

    def v_copy(slot):
        there = row_partner(row, slot, 1)
        return pltpu.make_async_remote_copy(
            src_ref=v_out.at[there],
            dst_ref=kv.at[0, slot, pl.ds(TOK, HALF)],
            send_sem=v_send.at[slot],
            recv_sem=v_recv.at[slot],
            device_id={"row": there},
            device_id_type=MESH,
        )

    def q_copy(slot):
        there = row_partner(row, slot, 1)
        return pltpu.make_async_remote_copy(
            src_ref=q_hbm.at[0, :, pl.ds(pl.multiple_of(there * HD, HD), HD)],
            dst_ref=q_ref.at[pl.ds(slot * TOK, TOK)],
            send_sem=q_send.at[slot],
            recv_sem=q_recv.at[slot],
            device_id={"row": there},
            device_id_type=MESH,
        )

    def hop_copy(kind, group):
        src, dst, there = (
            (0, 1, up),
            (0, 2, down),
            (0, 3, opposite),
            (0, 4, sibling),
            (1, 5, sibling),
            (2, 6, sibling),
            (3, 7, sibling),
        )[kind]
        part = pl.ds(group * PER_GROUP, PER_GROUP)
        return pltpu.make_async_remote_copy(
            src_ref=kv.at[src, part],
            dst_ref=kv.at[dst, part],
            send_sem=hop_send.at[kind, group],
            recv_sem=hop_recv.at[kind, group],
            device_id={"col": there},
            device_id_type=MESH,
        )

    def share_copy(slot):
        return pltpu.make_async_remote_copy(
            src_ref=sh_out.at[slot],
            dst_ref=sh_in.at[slot],
            send_sem=sh_send.at[slot],
            recv_sem=sh_recv.at[slot],
            device_id={"row": row_partner(row, slot, -1)},
            device_id_type=MESH,
        )

    def copy_to(side, tile):
        if tile == 4:
            src, dst = raw, raw_in
        else:
            src, dst = mine, around.at[side, 8 - tile]
        return pltpu.make_async_remote_copy(
            src_ref=src,
            dst_ref=dst,
            send_sem=send.at[side, tile],
            recv_sem=recv.at[side, tile],
            device_id=place(side, tile),
            device_id_type=MESH,
        )

    near, far = range(1, 2 * PER_GROUP), range(2 * PER_GROUP, SLOTS)
    pl.semaphore_wait(barrier, SLOTS - 1 + 4 + len(peers))
    for slot in near:
        k_copy(slot).start()
    for slot in near:
        q_copy(slot).start()

    loads[0].wait()
    loads[1].wait()
    for head in range(SLOTS):
        cols = slice(head * HD, (head + 1) * HD)
        projected = lax.dot_general(
            v_ref[:, cols], w_ref[:, cols], (((1,), (1,)), ((), ())), preferred_element_type=F32
        )
        v_out[head] = jnp.concatenate([projected[0:HALF], projected[HALF:TOK]], axis=1).astype(BF16)
    for slot in near:
        v_copy(slot).start()
    for slot in far:
        q_copy(slot).start()
    kv[0, 0, TOK:KV_ROWS, :] = v_out[row]

    w_copies = []
    for b in range(3):
        for c in range(3):
            for a in range(3):
                w_copies.append(
                    pltpu.make_async_copy(
                        wmid_hbm.at[a, b, c],
                        wmid.at[b * 3 + c, pl.ds(a * 512, 512)],
                        w_sem.at[(b * 3 + c) * 3 + a],
                    )
                )
    for copy in w_copies:
        copy.start()

    o_ref[...] = jnp.zeros_like(o_ref)
    m_ref[...] = jnp.full_like(m_ref, NEG_FILL)
    kv_lane = lax.broadcasted_iota(jnp.int32, (HALF, HD), 1)
    ones = jnp.where(kv_lane == HD // 2, 1.0, 0.0).astype(F32)

    def first_hop(group):
        for slot in range(group * PER_GROUP, (group + 1) * PER_GROUP):
            if slot:
                k_copy(slot).wait_recv()
                v_copy(slot).wait_recv()
        for kind in (0, 1, 2, 3):
            hop_copy(kind, group).start()

    def second_hop(group):
        for kind in (0, 1, 2):
            hop_copy(kind, group).wait_recv()
        for kind in (4, 5, 6):
            hop_copy(kind, group).start()

    def from_sibling(group):
        for kind in (3, 4, 5, 6):
            hop_copy(kind, group).wait_recv()

    for copy in loads[2:]:
        copy.wait()
    first_hop(0)

    cells = [
        (
            (f // 3) * 4 + p * 2 + s,
            pl.ds((f % 3) * PLACES + i * TCOLS, TCOLS),
            pl.ds(f * 64 + (2 * i + p) * 8 + s, TCOLS, stride=2),
        )
        for f in range(FRAMES)
        for i in range(TROWS)
        for p in range(2)
        for s in range(2)
    ]
    for piece, packed_rows, tile_rows in cells:
        pieces[piece, packed_rows, :] = lat_in[tile_rows, :]
    lat_ref[...] = jnp.concatenate([pieces[piece] for piece in range(8)], axis=1)

    zero = jnp.zeros((16, 512), BF16)
    for a in range(3):
        for r in range(4):
            for c in range(4):
                lanes = (((r // 2) * 2 + c // 2) * 4 + (r % 2) * 2 + c % 2) * 16
                for pp in range(2):
                    for ss in range(2):
                        inside = 0 <= r - pp < 3 and 0 <= c - ss < 3
                        w_in[
                            a * 256 + lanes : a * 256 + lanes + 16,
                            (pp * 2 + ss) * 512 : (pp * 2 + ss + 1) * 512,
                        ] = win_ref[a, r - pp, c - ss] if inside else zero

    text_rows = tk_ref.shape[0]
    text_projected = lax.dot_general(
        tv_ref[...], w_ref[:, head_cols], (((1,), (1,)), ((), ())), preferred_element_type=F32
    )
    text_lane = lax.broadcasted_iota(jnp.int32, (text_rows, HD // 2), 1)
    text_value[...] = jnp.concatenate(
        [text_projected, jnp.where(text_lane == 0, 1.0, 0.0).astype(F32)], axis=1
    ).astype(BF16)

    def attend_text(part):
        usable = lax.broadcasted_iota(jnp.int32, (PART, text_rows), 1) < len_ref[0]
        attend(q_ref, o_ref, m_ref, part, tk_ref, text_value, usable)

    def share_of(slot):
        out = o_ref[slot * TOK : (slot + 1) * TOK, :]
        share = out[:, 0 : HD // 2] / out[:, HD // 2 : HD // 2 + 1]
        return jnp.concatenate([share[0:HALF], share[HALF:TOK]], axis=1)

    def send_shares(slots):
        for slot in slots:
            sh_out[slot] = share_of(slot).astype(BF16)
            share_copy(slot).start()

    for slot in near:
        q_copy(slot).wait_recv()
    attend_text(0)
    second_hop(0)
    first_hop(1)

    def before_1():
        from_sibling(0)
        for slot in far[:PER_GROUP]:
            q_copy(slot).wait_send()
            k_copy(slot).start()
            v_copy(slot).start()

    def before_2():
        for slot in far[PER_GROUP:]:
            q_copy(slot).wait_send()
            k_copy(slot).start()
            v_copy(slot).start()
        for slot in far:
            q_copy(slot).wait_recv()
        attend_text(1)

    def before_3():
        second_hop(1)

    def before_5():
        first_hop(2)

    def before_6():
        from_sibling(1)

    def before_7():
        first_hop(3)

    def before_8():
        second_hop(2)

    def before_10():
        from_sibling(2)
        second_hop(3)

    def before_14():
        from_sibling(3)

    def before_15():
        send_shares(reversed(far))

    steps = {
        1: before_1,
        2: before_2,
        3: before_3,
        5: before_5,
        6: before_6,
        7: before_7,
        8: before_8,
        10: before_10,
        14: before_14,
        15: before_15,
    }

    @pl.loop(0, 4 * GROUPS)
    def _(unit):
        for when, step in steps.items():
            pl.when(unit == when)(step)
        opening = (19 - unit) // 16
        closing = (unit + 2) // 16
        even = 1 - unit % 2
        chunk = opening * (unit % 2) + (1 - opening) * (unit // 2)
        usual = (1 - closing) * (1 - even) + closing * even
        part = opening * (unit // 2) + (1 - opening) * usual
        fresh = opening * (1 - unit // 2) + (1 - opening) * even
        group, side, slab = chunk // 2, chunk % 2, chunk % 2

        @pl.when(fresh == 1)
        def _():
            for member in range(4):
                for slot in range(PER_GROUP):
                    at = (member * PER_GROUP + slot) * TOK
                    block = kv.at[4 * side + member, group * PER_GROUP + slot]
                    key_ref[slab, at : at + TOK, :] = block[0:TOK, :]
                    packed = block[TOK:KV_ROWS, :].astype(F32)
                    value_ref[slab, at : at + HALF, :] = jnp.where(
                        kv_lane < HD // 2, packed, ones
                    ).astype(BF16)
                    value_ref[slab, at + HALF : at + TOK, :] = jnp.where(
                        kv_lane < HD // 2, pltpu.roll(packed, HD // 2, 1), ones
                    ).astype(BF16)

        attend(q_ref, o_ref, m_ref, part, key_ref.at[slab], value_ref.at[slab], None)

    send_shares(reversed(near))
    velocity = share_of(0)
    for slot in range(1, SLOTS):
        share_copy(slot).wait_recv()
        velocity = velocity + sh_in[slot].astype(F32)

    index = step_ref[0].astype(F32)
    advance = sigma_at(index + 1.0) - sigma_at(index)
    first = branch == 0
    raw[...] = velocity
    keep = jnp.where(first, 1.0, 0.0)
    gain = jnp.where(first, COND_GAIN, UNCOND_GAIN) * advance
    mine[...] = lat_ref[...] * keep + velocity * gain
    for side, tile in peers:
        copy_to(side, tile).start()
    for side, tile in peers:
        copy_to(side, tile).wait_recv()

    cond = jnp.where(first, raw[...], raw_in[...])
    uncond = jnp.where(first, raw_in[...], raw[...])
    guided = COND_GAIN * cond + UNCOND_GAIN * uncond
    for piece in range(8):
        pieces[piece] = guided[:, piece * 16 : (piece + 1) * 16]
    for piece, packed_rows, tile_rows in cells:
        guided_ref[tile_rows, :] = pieces[piece, packed_rows, :]
    for tile, (dr, dc) in enumerate(AROUND):
        if tile == 4:
            value = lat_ref[...] + advance * guided
        else:
            there_row, there_col = row + dr, col + dc
            there = (
                (there_row >= 0)
                & (there_row < row_count)
                & (there_col >= 0)
                & (there_col < col_count)
            )
            value = (around[0, tile] + around[1, tile]) * jnp.where(there, 1.0, 0.0)
        moved[tile * HALF : (tile + 1) * HALF, :] = value.astype(BF16)

    picked = jnp.dot(pick_ref[...], moved[...], preferred_element_type=F32)
    lane = lax.broadcasted_iota(jnp.int32, (HALF, HD), 1)
    low = lane < HD // 2
    for e in range(3):
        for g in range(2):
            at = (e * 3 + g) * HALF
            here, right = picked[at : at + HALF], picked[at + HALF : at + 2 * HALF]
            early = jnp.where(low, here, pltpu.roll(right, HD // 2, 1)).astype(BF16)
            late = jnp.where(low, pltpu.roll(here, HD // 2, 1), right).astype(BF16)
            shifted[e, g, 0:PLACES, :] = early[0:PLACES]
            shifted[e, g, PLACES : 2 * PLACES, :] = early[0:PLACES]
            shifted[e, g, 2 * PLACES : 2 * PLACES + HALF, :] = early
            shifted[e, g, 2 * PLACES + HALF : PADDED_ROWS, :] = late

    patches = jnp.concatenate(
        [
            jnp.concatenate(
                [
                    shifted[db + du, dc, a * PLACES : a * PLACES + ROWS, :]
                    for a in range(3)
                    for du in range(2)
                ],
                axis=1,
            )
            for db in range(2)
            for dc in range(2)
        ],
        axis=0,
    )

    at = lax.broadcasted_iota(jnp.int32, (ROWS, 1), 0)
    row_at, col_at = (at // TCOLS) % TROWS, at % TCOLS
    bias_in = bin_ref[...]
    for pp in range(2):
        for ss in range(2):
            kind = pp * 2 + ss
            for half in range(2):
                cols = slice(half * 256, (half + 1) * 256)
                hidden = (
                    jnp.dot(
                        patches,
                        w_in[:, kind * 512 + half * 256 : kind * 512 + (half + 1) * 256],
                        preferred_element_type=F32,
                    )
                    + bias_in[:, cols]
                )
                for db in range(2):
                    for dc in range(2):
                        shift = db * 2 + dc
                        block = hidden[shift * ROWS : (shift + 1) * ROWS]
                        if (db, dc) == (1 - pp, 1 - ss):
                            center[kind, :, cols] = block
                        y_at = row * (2 * TROWS) - 1 + 2 * (row_at + db) + pp
                        x_at = col * (2 * TCOLS) - 1 + 2 * (col_at + dc) + ss
                        inside = (
                            (y_at >= 0)
                            & (y_at < row_count * 2 * TROWS)
                            & (x_at >= 0)
                            & (x_at < col_count * 2 * TCOLS)
                        )
                        value = jnp.where(inside, block * jax.nn.sigmoid(block), 0.0).astype(BF16)
                        act[kind, shift, 0:PLACES, cols] = value[0:PLACES]
                        act[kind, shift, PLACES : 2 * PLACES, cols] = value[0:PLACES]
                        act[kind, shift, 2 * PLACES : PADDED_ROWS, cols] = value

    total = None
    for b in range(3):
        for c in range(3):
            for a in range(3):
                w_copies[(b * 3 + c) * 3 + a].wait()
            window = []
            for pi in range(2):
                for si in range(2):
                    kind = ((pi + b) % 2) * 2 + (si + c) % 2
                    shift = ((pi + b) // 2) * 2 + (si + c) // 2
                    window.append(
                        jnp.concatenate(
                            [
                                act[kind, shift, a * PLACES : a * PLACES + ROWS, :]
                                for a in range(3)
                            ],
                            axis=1,
                        )
                    )
            term = jnp.dot(
                jnp.concatenate(window, axis=0), wmid[b * 3 + c], preferred_element_type=F32
            )
            total = term if total is None else total + term
    own = pl.ds(pl.multiple_of(branch * 256, 256), 256)
    for pi in range(2):
        for si in range(2):
            phase = pi * 2 + si
            result = (
                center[(1 - pi) * 2 + (1 - si), :, own]
                + total[phase * ROWS : (phase + 1) * ROWS]
                + bmid_ref[...]
            )
            for f in range(FRAMES):
                for i in range(TROWS):
                    at = f * PLACES + i * TCOLS
                    tile_rows = pl.ds(f * 64 + (2 * i + pi) * 8 + si, TCOLS, stride=2)
                    for side in range(2):
                        ordered[side, tile_rows, :] = result[
                            at : at + TCOLS, side * 128 : (side + 1) * 128
                        ]
    for side in range(2):
        out_ref[:, side * 128 : (side + 1) * 128] = ordered[side]

    for side, tile in peers:
        copy_to(side, tile).wait_send()
    for slot in range(1, SLOTS):
        k_copy(slot).wait_send()
        v_copy(slot).wait_send()
        if slot in near:
            q_copy(slot).wait_send()
        share_copy(slot).wait_send()
    for group in range(GROUPS):
        for kind in range(7):
            hop_copy(kind, group).wait_send()


def step(
    row_count, col_count,
    queries, keys, values, out_proj, text_keys, text_values, text_lengths,
    latent_cells, step_index, w_in, b_in, w_mid, b_mid,
):
    text_rows = text_keys.shape[1]
    vmem = pl.BlockSpec(memory_space=pltpu.VMEM)
    smem = pl.BlockSpec(memory_space=pltpu.SMEM)
    hbm = pl.BlockSpec(memory_space=pltpu.HBM)
    dma = pltpu.SemaphoreType.DMA
    return pl.pallas_call(
        functools.partial(step_kernel, row_count, col_count),
        out_shape=(
            jax.ShapeDtypeStruct((4 * ROWS, 16), F32),
            jax.ShapeDtypeStruct((4 * ROWS, 256), F32),
        ),
        in_specs=[hbm] * 6 + [smem] + [hbm] * 2 + [smem] + [hbm] * 4,
        out_specs=(vmem, vmem),
        scratch_shapes=[
            pltpu.VMEM((TOK, SLOTS * HD), BF16),
            pltpu.VMEM((HD // 2, SLOTS * HD), BF16),
            pltpu.VMEM((SLOTS, HALF, HD), BF16),
            pltpu.VMEM((8, SLOTS, KV_ROWS, HD), BF16),
            pltpu.VMEM((QUERIES, HD), BF16),
            pltpu.VMEM((QUERIES, HD), F32),
            pltpu.VMEM((QUERIES, HD), F32),
            pltpu.VMEM((2, CHUNK, HD), BF16),
            pltpu.VMEM((2, CHUNK, HD), BF16),
            pltpu.VMEM((text_rows, HD), BF16),
            pltpu.VMEM((text_rows, HD), BF16),
            pltpu.VMEM((text_rows, HD), BF16),
            pltpu.VMEM((SLOTS, HALF, HD), BF16),
            pltpu.VMEM((SLOTS, HALF, HD), BF16),
            pltpu.VMEM((4 * ROWS, 16), F32),
            pltpu.VMEM((8, HALF, 16), F32),
            pltpu.VMEM((HALF, HD), F32),
            pltpu.VMEM((9 * HALF, 9 * HALF), BF16),
            pltpu.VMEM((3, 3, 3, 16, 512), BF16),
            pltpu.VMEM((1, 512), F32),
            pltpu.VMEM((1, 256), F32),
            pltpu.VMEM((HALF, HD), F32),
            pltpu.VMEM((HALF, HD), F32),
            pltpu.VMEM((HALF, HD), F32),
            pltpu.VMEM((2, 9, HALF, HD), F32),
            pltpu.VMEM((9 * HALF, HD), BF16),
            pltpu.VMEM((3, 2, PADDED_ROWS, HD), BF16),
            pltpu.VMEM((768, 2048), BF16),
            pltpu.VMEM((9, 1536, 256), BF16),
            pltpu.VMEM((4, 4, PADDED_ROWS, 512), BF16),
            pltpu.VMEM((4, ROWS, 512), F32),
            pltpu.VMEM((2, 4 * ROWS, 128), F32),
            dma((SLOTS,)), dma((SLOTS,)), dma((SLOTS,)), dma((SLOTS,)), dma((SLOTS,)), dma((SLOTS,)),
            dma((7, GROUPS)), dma((7, GROUPS)), dma((SLOTS,)), dma((SLOTS,)),
            dma((2, 9)), dma((2, 9)), dma((27,)), dma((11,)),
        ],
        compiler_params=pltpu.CompilerParams(
            collective_id=0, has_side_effects=True, vmem_limit_bytes=58 * 2**20
        ),
        name="step",
    )(
        queries, keys, values, out_proj.T, text_keys, text_values, text_lengths,
        latent_cells, jnp.asarray(pick_matrix(), BF16), step_index,
        w_in, b_in[None, :], w_mid, b_mid[None, :],
    )


def local(
    row_count,
    col_count,
    queries,
    keys,
    values,
    text_keys,
    text_values,
    text_lengths,
    step_index,
    out_proj,
    latent,
    conv_in_w,
    conv_in_b,
    conv_mid_w,
    conv_mid_b,
):
    guided, decoded = step(
        row_count, col_count,
        queries, keys, values, out_proj, text_keys, text_values, text_lengths,
        latent.reshape(-1, 16), step_index, conv_in_w, conv_in_b, conv_mid_w, conv_mid_b,
    )
    return guided.reshape(latent.shape), decoded.reshape(latent.shape[:3] + (-1,))


def solution(mesh):
    return jax.shard_map(
        functools.partial(local, mesh.shape["row"], mesh.shape["col"]),
        mesh=mesh,
        in_specs=(
            P("branch", ("row", "col"), None),
            P("branch", ("row", "col"), None),
            P("branch", ("row", "col"), None),
            P("branch", None, None),
            P("branch", None, None),
            P("branch"),
            P(),
            P(),
            P(None, "row", "col", None),
            P(),
            P(),
            P(None, None, None, None, "branch"),
            P("branch"),
        ),
        out_specs=(P(None, "row", "col", None), P(None, "row", "col", "branch")),
        check_vma=False,
    )
```

```python
import functools

import jax
import jax.numpy as jnp
import numpy as np
from jax import lax
from jax.experimental import pallas as pl
from jax.experimental.pallas import tpu as pltpu
from jax.sharding import PartitionSpec as P

HD = 128
MESH = pl.DeviceIdType.MESH
NEG_FILL = -1e30
COND_GAIN = 6.0
UNCOND_GAIN = -5.0
SCORE_GAIN = float(HD**-0.5 * np.log2(np.e))

Z_ORDER = (0, 1, 7, 2, 6, 3, 5, 4)
Z_COUNT = 8
SLOTS = 16
TOK = 96
HALF = 48
KV_ROWS = TOK + HALF
GROUPS = 4
PER_GROUP = 4
QUERIES = SLOTS * TOK
CHUNK = 4 * PER_GROUP * TOK
PART = QUERIES // 2

BF16 = jnp.bfloat16
F32 = jnp.float32


def row_partner(row, slot, sign):
    z, x = row // 2, row % 2
    dz = Z_ORDER[slot // 2]
    dz = dz if sign > 0 else (Z_COUNT - dz) % Z_COUNT
    return lax.rem(z + dz, Z_COUNT) * 2 + lax.rem(x + slot % 2, 2)


AROUND = tuple((dr, dc) for dr in (-1, 0, 1) for dc in (-1, 0, 1))
FRAMES, TROWS, TCOLS = 6, 4, 4
PLACES = TROWS * TCOLS
ROWS = FRAMES * PLACES
PADDED_ROWS = (FRAMES + 2) * PLACES


def pick_matrix():
    pick = np.zeros((3, 3, FRAMES // 2, TROWS, TCOLS, 9, FRAMES // 2, TROWS, TCOLS), np.float32)
    for e, g, f, i, j in np.ndindex(3, 3, FRAMES // 2, TROWS, TCOLS):
        r, c = i + e - 1, j + g - 1
        tile = AROUND.index((r // TROWS, c // TCOLS))
        pick[e, g, f, i, j, tile, f, r % TROWS, c % TCOLS] = 1.0
    return pick.reshape(9 * HALF, 9 * HALF)


def sigma_at(index):
    s = 1.0 - index / 50.0
    return 7.0 * s / (1.0 + 6.0 * s)


def attend(q_ref, o_ref, m_ref, part, key_ref, value_ref, usable):
    rows = pl.ds(pl.multiple_of(part * PART, PART), PART)
    scores = lax.dot_general(
        q_ref[rows, :], key_ref[...], (((1,), (1,)), ((), ())), preferred_element_type=F32
    )
    if usable is not None:
        scores = jnp.where(usable, scores, NEG_FILL)
    before = m_ref[rows, :]
    top = jnp.maximum(before, jnp.max(scores, axis=1, keepdims=True) * SCORE_GAIN)
    wide = jnp.concatenate([top] * (scores.shape[1] // HD), axis=1)
    weights = jnp.exp2(scores * SCORE_GAIN - wide).astype(BF16)
    o_ref[rows, :] = o_ref[rows, :] * jnp.exp2(before - top) + jnp.dot(
        weights, value_ref[...], preferred_element_type=F32
    )
    m_ref[rows, :] = top


def step_kernel(
    row_count, col_count,
    q_hbm, k_hbm, v_hbm, w_hbm, tk_hbm, tv_hbm, len_ref,
    lat_hbm, pick_hbm, step_ref, win_hbm, bin_hbm, wmid_hbm, bmid_hbm,
    guided_ref, out_ref,
    v_ref, w_ref, v_out, kv, q_ref, o_ref, m_ref, key_ref, value_ref, tk_ref, tv_ref, text_value, sh_out, sh_in,
    lat_in, pieces, lat_ref, pick_ref, win_ref, bin_ref, bmid_ref,
    mine, raw, raw_in, around, moved, shifted, w_in, wmid, act, center, ordered,
    k_send, k_recv, v_send, v_recv, q_send, q_recv, hop_send, hop_recv, sh_send, sh_recv,
    send, recv, w_sem, in_sem,
):
    branch, row, col = lax.axis_index("branch"), lax.axis_index("row"), lax.axis_index("col")
    y, core = col // 2, col % 2
    up = lax.rem(y + 1, 4) * 2 + core
    down = lax.rem(y + 3, 4) * 2 + core
    opposite = lax.rem(y + 2, 4) * 2 + core
    sibling = y * 2 + 1 - core

    def place(side, tile):
        dr, dc = AROUND[tile]
        return {
            "branch": lax.rem(branch + side, 2),
            "row": lax.rem(row + dr + row_count, row_count),
            "col": lax.rem(col + dc + col_count, col_count),
        }

    peers = [(side, tile) for side in (0, 1) for tile in range(9) if (side, tile) != (0, 4)]

    barrier = pltpu.get_barrier_semaphore()
    for slot in range(1, SLOTS):
        pl.semaphore_signal(
            barrier, inc=1, device_id={"row": row_partner(row, slot, 1)}, device_id_type=MESH
        )
    for other in (up, down, opposite, sibling):
        pl.semaphore_signal(barrier, inc=1, device_id={"col": other}, device_id_type=MESH)
    for side, tile in peers:
        pl.semaphore_signal(barrier, inc=1, device_id=place(side, tile), device_id_type=MESH)

    head_cols = pl.ds(pl.multiple_of(row * HD, HD), HD)
    loads = [
        pltpu.make_async_copy(src, dst, in_sem.at[i])
        for i, (src, dst) in enumerate(
            (
                (v_hbm.at[0], v_ref),
                (w_hbm, w_ref),
                (k_hbm.at[0, :, head_cols], kv.at[0, 0, pl.ds(0, TOK)]),
                (q_hbm.at[0, :, head_cols], q_ref.at[pl.ds(0, TOK)]),
                (tk_hbm.at[0, :, head_cols], tk_ref),
                (tv_hbm.at[0, :, head_cols], tv_ref),
                (win_hbm, win_ref),
                (bin_hbm, bin_ref),
                (bmid_hbm, bmid_ref),
                (pick_hbm, pick_ref),
                (lat_hbm, lat_in),
            )
        )
    ]
    for copy in loads:
        copy.start()

    def k_copy(slot):
        there = row_partner(row, slot, 1)
        return pltpu.make_async_remote_copy(
            src_ref=k_hbm.at[0, :, pl.ds(pl.multiple_of(there * HD, HD), HD)],
            dst_ref=kv.at[0, slot, pl.ds(0, TOK)],
            send_sem=k_send.at[slot],
            recv_sem=k_recv.at[slot],
            device_id={"row": there},
            device_id_type=MESH,
        )

    def v_copy(slot):
        there = row_partner(row, slot, 1)
        return pltpu.make_async_remote_copy(
            src_ref=v_out.at[there],
            dst_ref=kv.at[0, slot, pl.ds(TOK, HALF)],
            send_sem=v_send.at[slot],
            recv_sem=v_recv.at[slot],
            device_id={"row": there},
            device_id_type=MESH,
        )

    def q_copy(slot):
        there = row_partner(row, slot, 1)
        return pltpu.make_async_remote_copy(
            src_ref=q_hbm.at[0, :, pl.ds(pl.multiple_of(there * HD, HD), HD)],
            dst_ref=q_ref.at[pl.ds(slot * TOK, TOK)],
            send_sem=q_send.at[slot],
            recv_sem=q_recv.at[slot],
            device_id={"row": there},
            device_id_type=MESH,
        )

    def hop_copy(kind, group):
        src, dst, there = (
            (0, 1, up),
            (0, 2, down),
            (0, 3, opposite),
            (0, 4, sibling),
            (1, 5, sibling),
            (2, 6, sibling),
            (3, 7, sibling),
        )[kind]
        part = pl.ds(group * PER_GROUP, PER_GROUP)
        return pltpu.make_async_remote_copy(
            src_ref=kv.at[src, part],
            dst_ref=kv.at[dst, part],
            send_sem=hop_send.at[kind, group],
            recv_sem=hop_recv.at[kind, group],
            device_id={"col": there},
            device_id_type=MESH,
        )

    def share_copy(slot):
        return pltpu.make_async_remote_copy(
            src_ref=sh_out.at[slot],
            dst_ref=sh_in.at[slot],
            send_sem=sh_send.at[slot],
            recv_sem=sh_recv.at[slot],
            device_id={"row": row_partner(row, slot, -1)},
            device_id_type=MESH,
        )

    def copy_to(side, tile):
        if tile == 4:
            src, dst = raw, raw_in
        else:
            src, dst = mine, around.at[side, 8 - tile]
        return pltpu.make_async_remote_copy(
            src_ref=src,
            dst_ref=dst,
            send_sem=send.at[side, tile],
            recv_sem=recv.at[side, tile],
            device_id=place(side, tile),
            device_id_type=MESH,
        )

    near, far = range(1, 2 * PER_GROUP), range(2 * PER_GROUP, SLOTS)
    pl.semaphore_wait(barrier, SLOTS - 1 + 4 + len(peers))
    for slot in near:
        k_copy(slot).start()
    for slot in near:
        q_copy(slot).start()

    loads[0].wait()
    loads[1].wait()
    for head in range(SLOTS):
        cols = slice(head * HD, (head + 1) * HD)
        projected = lax.dot_general(
            v_ref[:, cols], w_ref[:, cols], (((1,), (1,)), ((), ())), preferred_element_type=F32
        )
        v_out[head] = jnp.concatenate([projected[0:HALF], projected[HALF:TOK]], axis=1).astype(BF16)
    for slot in near:
        v_copy(slot).start()
    for slot in far[:PER_GROUP]:
        k_copy(slot).start()
        v_copy(slot).start()
    for slot in far:
        q_copy(slot).start()
    for slot in far[PER_GROUP:]:
        k_copy(slot).start()
        v_copy(slot).start()
    kv[0, 0, TOK:KV_ROWS, :] = v_out[row]

    w_copies = []
    for b in range(3):
        for c in range(3):
            for a in range(3):
                w_copies.append(
                    pltpu.make_async_copy(
                        wmid_hbm.at[a, b, c],
                        wmid.at[b * 3 + c, pl.ds(a * 512, 512)],
                        w_sem.at[(b * 3 + c) * 3 + a],
                    )
                )
    for copy in w_copies:
        copy.start()

    o_ref[...] = jnp.zeros_like(o_ref)
    m_ref[...] = jnp.full_like(m_ref, NEG_FILL)
    kv_lane = lax.broadcasted_iota(jnp.int32, (HALF, HD), 1)
    ones = jnp.where(kv_lane == HD // 2, 1.0, 0.0).astype(F32)

    def first_hop(group):
        for slot in range(group * PER_GROUP, (group + 1) * PER_GROUP):
            if slot:
                k_copy(slot).wait_recv()
                v_copy(slot).wait_recv()
        for kind in (0, 1, 2, 3):
            hop_copy(kind, group).start()

    def second_hop(group):
        for kind in (0, 1, 2):
            hop_copy(kind, group).wait_recv()
        for kind in (4, 5, 6):
            hop_copy(kind, group).start()

    def from_sibling(group):
        for kind in (3, 4, 5, 6):
            hop_copy(kind, group).wait_recv()

    for copy in loads[2:]:
        copy.wait()
    first_hop(0)
    first_hop(1)

    cells = [
        (
            (f // 3) * 4 + p * 2 + s,
            pl.ds((f % 3) * PLACES + i * TCOLS, TCOLS),
            pl.ds(f * 64 + (2 * i + p) * 8 + s, TCOLS, stride=2),
        )
        for f in range(FRAMES)
        for i in range(TROWS)
        for p in range(2)
        for s in range(2)
    ]
    for piece, packed_rows, tile_rows in cells:
        pieces[piece, packed_rows, :] = lat_in[tile_rows, :]
    lat_ref[...] = jnp.concatenate([pieces[piece] for piece in range(8)], axis=1)

    zero = jnp.zeros((16, 512), BF16)
    for a in range(3):
        for r in range(4):
            for c in range(4):
                lanes = (((r // 2) * 2 + c // 2) * 4 + (r % 2) * 2 + c % 2) * 16
                for pp in range(2):
                    for ss in range(2):
                        inside = 0 <= r - pp < 3 and 0 <= c - ss < 3
                        w_in[
                            a * 256 + lanes : a * 256 + lanes + 16,
                            (pp * 2 + ss) * 512 : (pp * 2 + ss + 1) * 512,
                        ] = win_ref[a, r - pp, c - ss] if inside else zero

    text_rows = tk_ref.shape[0]
    text_projected = lax.dot_general(
        tv_ref[...], w_ref[:, head_cols], (((1,), (1,)), ((), ())), preferred_element_type=F32
    )
    text_lane = lax.broadcasted_iota(jnp.int32, (text_rows, HD // 2), 1)
    text_value[...] = jnp.concatenate(
        [text_projected, jnp.where(text_lane == 0, 1.0, 0.0).astype(F32)], axis=1
    ).astype(BF16)

    def attend_text(part):
        usable = lax.broadcasted_iota(jnp.int32, (PART, text_rows), 1) < len_ref[0]
        attend(q_ref, o_ref, m_ref, part, tk_ref, text_value, usable)

    def share_of(slot):
        out = o_ref[slot * TOK : (slot + 1) * TOK, :]
        share = out[:, 0 : HD // 2] / out[:, HD // 2 : HD // 2 + 1]
        return jnp.concatenate([share[0:HALF], share[HALF:TOK]], axis=1)

    def send_shares(slots):
        for slot in slots:
            sh_out[slot] = share_of(slot).astype(BF16)
            share_copy(slot).start()

    for slot in near:
        q_copy(slot).wait_recv()
    attend_text(0)
    second_hop(0)

    def before_1():
        from_sibling(0)

    def before_2():
        for slot in far:
            q_copy(slot).wait_recv()
        attend_text(1)
        second_hop(1)
        first_hop(2)

    def before_4():
        first_hop(3)

    def before_6():
        from_sibling(1)

    def before_7():
        second_hop(2)

    def before_9():
        second_hop(3)

    def before_10():
        from_sibling(2)

    def before_14():
        from_sibling(3)

    def before_15():
        send_shares(reversed(far))

    steps = {
        1: before_1,
        2: before_2,
        4: before_4,
        6: before_6,
        7: before_7,
        9: before_9,
        10: before_10,
        14: before_14,
        15: before_15,
    }

    @pl.loop(0, 4 * GROUPS)
    def _(unit):
        for when, step in steps.items():
            pl.when(unit == when)(step)
        opening = (19 - unit) // 16
        closing = (unit + 2) // 16
        even = 1 - unit % 2
        chunk = opening * (unit % 2) + (1 - opening) * (unit // 2)
        usual = (1 - closing) * (1 - even) + closing * even
        part = opening * (unit // 2) + (1 - opening) * usual
        fresh = opening * (1 - unit // 2) + (1 - opening) * even
        group, side, slab = chunk // 2, chunk % 2, chunk % 2

        @pl.when(fresh == 1)
        def _():
            for member in range(4):
                for slot in range(PER_GROUP):
                    at = (member * PER_GROUP + slot) * TOK
                    block = kv.at[4 * side + member, group * PER_GROUP + slot]
                    key_ref[slab, at : at + TOK, :] = block[0:TOK, :]
                    packed = block[TOK:KV_ROWS, :].astype(F32)
                    value_ref[slab, at : at + HALF, :] = jnp.where(
                        kv_lane < HD // 2, packed, ones
                    ).astype(BF16)
                    value_ref[slab, at + HALF : at + TOK, :] = jnp.where(
                        kv_lane < HD // 2, pltpu.roll(packed, HD // 2, 1), ones
                    ).astype(BF16)

        attend(q_ref, o_ref, m_ref, part, key_ref.at[slab], value_ref.at[slab], None)

    send_shares(reversed(near))
    velocity = share_of(0)
    for slot in range(1, SLOTS):
        share_copy(slot).wait_recv()
        velocity = velocity + sh_in[slot].astype(F32)

    index = step_ref[0].astype(F32)
    advance = sigma_at(index + 1.0) - sigma_at(index)
    first = branch == 0
    raw[...] = velocity
    keep = jnp.where(first, 1.0, 0.0)
    gain = jnp.where(first, COND_GAIN, UNCOND_GAIN) * advance
    mine[...] = lat_ref[...] * keep + velocity * gain
    for side, tile in peers:
        copy_to(side, tile).start()
    for side, tile in peers:
        copy_to(side, tile).wait_recv()

    cond = jnp.where(first, raw[...], raw_in[...])
    uncond = jnp.where(first, raw_in[...], raw[...])
    guided = COND_GAIN * cond + UNCOND_GAIN * uncond
    for piece in range(8):
        pieces[piece] = guided[:, piece * 16 : (piece + 1) * 16]
    for piece, packed_rows, tile_rows in cells:
        guided_ref[tile_rows, :] = pieces[piece, packed_rows, :]
    for tile, (dr, dc) in enumerate(AROUND):
        if tile == 4:
            value = lat_ref[...] + advance * guided
        else:
            there_row, there_col = row + dr, col + dc
            there = (
                (there_row >= 0)
                & (there_row < row_count)
                & (there_col >= 0)
                & (there_col < col_count)
            )
            value = (around[0, tile] + around[1, tile]) * jnp.where(there, 1.0, 0.0)
        moved[tile * HALF : (tile + 1) * HALF, :] = value.astype(BF16)

    picked = jnp.dot(pick_ref[...], moved[...], preferred_element_type=F32)
    lane = lax.broadcasted_iota(jnp.int32, (HALF, HD), 1)
    low = lane < HD // 2
    for e in range(3):
        for g in range(2):
            at = (e * 3 + g) * HALF
            here, right = picked[at : at + HALF], picked[at + HALF : at + 2 * HALF]
            early = jnp.where(low, here, pltpu.roll(right, HD // 2, 1)).astype(BF16)
            late = jnp.where(low, pltpu.roll(here, HD // 2, 1), right).astype(BF16)
            shifted[e, g, 0:PLACES, :] = early[0:PLACES]
            shifted[e, g, PLACES : 2 * PLACES, :] = early[0:PLACES]
            shifted[e, g, 2 * PLACES : 2 * PLACES + HALF, :] = early
            shifted[e, g, 2 * PLACES + HALF : PADDED_ROWS, :] = late

    patches = jnp.concatenate(
        [
            jnp.concatenate(
                [
                    shifted[db + du, dc, a * PLACES : a * PLACES + ROWS, :]
                    for a in range(3)
                    for du in range(2)
                ],
                axis=1,
            )
            for db in range(2)
            for dc in range(2)
        ],
        axis=0,
    )

    at = lax.broadcasted_iota(jnp.int32, (ROWS, 1), 0)
    row_at, col_at = (at // TCOLS) % TROWS, at % TCOLS
    bias_in = bin_ref[...]
    for pp in range(2):
        for ss in range(2):
            kind = pp * 2 + ss
            for half in range(2):
                cols = slice(half * 256, (half + 1) * 256)
                hidden = (
                    jnp.dot(
                        patches,
                        w_in[:, kind * 512 + half * 256 : kind * 512 + (half + 1) * 256],
                        preferred_element_type=F32,
                    )
                    + bias_in[:, cols]
                )
                for db in range(2):
                    for dc in range(2):
                        shift = db * 2 + dc
                        block = hidden[shift * ROWS : (shift + 1) * ROWS]
                        if (db, dc) == (1 - pp, 1 - ss):
                            center[kind, :, cols] = block
                        y_at = row * (2 * TROWS) - 1 + 2 * (row_at + db) + pp
                        x_at = col * (2 * TCOLS) - 1 + 2 * (col_at + dc) + ss
                        inside = (
                            (y_at >= 0)
                            & (y_at < row_count * 2 * TROWS)
                            & (x_at >= 0)
                            & (x_at < col_count * 2 * TCOLS)
                        )
                        value = jnp.where(inside, block * jax.nn.sigmoid(block), 0.0).astype(BF16)
                        act[kind, shift, 0:PLACES, cols] = value[0:PLACES]
                        act[kind, shift, PLACES : 2 * PLACES, cols] = value[0:PLACES]
                        act[kind, shift, 2 * PLACES : PADDED_ROWS, cols] = value

    total = None
    for b in range(3):
        for c in range(3):
            for a in range(3):
                w_copies[(b * 3 + c) * 3 + a].wait()
            window = []
            for pi in range(2):
                for si in range(2):
                    kind = ((pi + b) % 2) * 2 + (si + c) % 2
                    shift = ((pi + b) // 2) * 2 + (si + c) // 2
                    window.append(
                        jnp.concatenate(
                            [
                                act[kind, shift, a * PLACES : a * PLACES + ROWS, :]
                                for a in range(3)
                            ],
                            axis=1,
                        )
                    )
            term = jnp.dot(
                jnp.concatenate(window, axis=0), wmid[b * 3 + c], preferred_element_type=F32
            )
            total = term if total is None else total + term
    own = pl.ds(pl.multiple_of(branch * 256, 256), 256)
    for pi in range(2):
        for si in range(2):
            phase = pi * 2 + si
            result = (
                center[(1 - pi) * 2 + (1 - si), :, own]
                + total[phase * ROWS : (phase + 1) * ROWS]
                + bmid_ref[...]
            )
            for f in range(FRAMES):
                for i in range(TROWS):
                    at = f * PLACES + i * TCOLS
                    tile_rows = pl.ds(f * 64 + (2 * i + pi) * 8 + si, TCOLS, stride=2)
                    for side in range(2):
                        ordered[side, tile_rows, :] = result[
                            at : at + TCOLS, side * 128 : (side + 1) * 128
                        ]
    for side in range(2):
        out_ref[:, side * 128 : (side + 1) * 128] = ordered[side]

    for side, tile in peers:
        copy_to(side, tile).wait_send()
    for slot in range(1, SLOTS):
        k_copy(slot).wait_send()
        v_copy(slot).wait_send()
        q_copy(slot).wait_send()
        share_copy(slot).wait_send()
    for group in range(GROUPS):
        for kind in range(7):
            hop_copy(kind, group).wait_send()


def step(
    row_count, col_count,
    queries, keys, values, out_proj, text_keys, text_values, text_lengths,
    latent_cells, step_index, w_in, b_in, w_mid, b_mid,
):
    text_rows = text_keys.shape[1]
    vmem = pl.BlockSpec(memory_space=pltpu.VMEM)
    smem = pl.BlockSpec(memory_space=pltpu.SMEM)
    hbm = pl.BlockSpec(memory_space=pltpu.HBM)
    dma = pltpu.SemaphoreType.DMA
    return pl.pallas_call(
        functools.partial(step_kernel, row_count, col_count),
        out_shape=(
            jax.ShapeDtypeStruct((4 * ROWS, 16), F32),
            jax.ShapeDtypeStruct((4 * ROWS, 256), F32),
        ),
        in_specs=[hbm] * 6 + [smem] + [hbm] * 2 + [smem] + [hbm] * 4,
        out_specs=(vmem, vmem),
        scratch_shapes=[
            pltpu.VMEM((TOK, SLOTS * HD), BF16),
            pltpu.VMEM((HD // 2, SLOTS * HD), BF16),
            pltpu.VMEM((SLOTS, HALF, HD), BF16),
            pltpu.VMEM((8, SLOTS, KV_ROWS, HD), BF16),
            pltpu.VMEM((QUERIES, HD), BF16),
            pltpu.VMEM((QUERIES, HD), F32),
            pltpu.VMEM((QUERIES, HD), F32),
            pltpu.VMEM((2, CHUNK, HD), BF16),
            pltpu.VMEM((2, CHUNK, HD), BF16),
            pltpu.VMEM((text_rows, HD), BF16),
            pltpu.VMEM((text_rows, HD), BF16),
            pltpu.VMEM((text_rows, HD), BF16),
            pltpu.VMEM((SLOTS, HALF, HD), BF16),
            pltpu.VMEM((SLOTS, HALF, HD), BF16),
            pltpu.VMEM((4 * ROWS, 16), F32),
            pltpu.VMEM((8, HALF, 16), F32),
            pltpu.VMEM((HALF, HD), F32),
            pltpu.VMEM((9 * HALF, 9 * HALF), BF16),
            pltpu.VMEM((3, 3, 3, 16, 512), BF16),
            pltpu.VMEM((1, 512), F32),
            pltpu.VMEM((1, 256), F32),
            pltpu.VMEM((HALF, HD), F32),
            pltpu.VMEM((HALF, HD), F32),
            pltpu.VMEM((HALF, HD), F32),
            pltpu.VMEM((2, 9, HALF, HD), F32),
            pltpu.VMEM((9 * HALF, HD), BF16),
            pltpu.VMEM((3, 2, PADDED_ROWS, HD), BF16),
            pltpu.VMEM((768, 2048), BF16),
            pltpu.VMEM((9, 1536, 256), BF16),
            pltpu.VMEM((4, 4, PADDED_ROWS, 512), BF16),
            pltpu.VMEM((4, ROWS, 512), F32),
            pltpu.VMEM((2, 4 * ROWS, 128), F32),
            dma((SLOTS,)), dma((SLOTS,)), dma((SLOTS,)), dma((SLOTS,)), dma((SLOTS,)), dma((SLOTS,)),
            dma((7, GROUPS)), dma((7, GROUPS)), dma((SLOTS,)), dma((SLOTS,)),
            dma((2, 9)), dma((2, 9)), dma((27,)), dma((11,)),
        ],
        compiler_params=pltpu.CompilerParams(
            collective_id=0, has_side_effects=True, vmem_limit_bytes=58 * 2**20
        ),
        name="step",
    )(
        queries, keys, values, out_proj.T, text_keys, text_values, text_lengths,
        latent_cells, jnp.asarray(pick_matrix(), BF16), step_index,
        w_in, b_in[None, :], w_mid, b_mid[None, :],
    )


def local(
    row_count,
    col_count,
    queries,
    keys,
    values,
    text_keys,
    text_values,
    text_lengths,
    step_index,
    out_proj,
    latent,
    conv_in_w,
    conv_in_b,
    conv_mid_w,
    conv_mid_b,
):
    guided, decoded = step(
        row_count, col_count,
        queries, keys, values, out_proj, text_keys, text_values, text_lengths,
        latent.reshape(-1, 16), step_index, conv_in_w, conv_in_b, conv_mid_w, conv_mid_b,
    )
    return guided.reshape(latent.shape), decoded.reshape(latent.shape[:3] + (-1,))


def solution(mesh):
    return jax.shard_map(
        functools.partial(local, mesh.shape["row"], mesh.shape["col"]),
        mesh=mesh,
        in_specs=(
            P("branch", ("row", "col"), None),
            P("branch", ("row", "col"), None),
            P("branch", ("row", "col"), None),
            P("branch", None, None),
            P("branch", None, None),
            P("branch"),
            P(),
            P(),
            P(None, "row", "col", None),
            P(),
            P(),
            P(None, None, None, None, "branch"),
            P("branch"),
        ),
        out_specs=(P(None, "row", "col", None), P(None, "row", "col", "branch")),
        check_vma=False,
    )
```

```python
import functools

import jax
import jax.numpy as jnp
import numpy as np
from jax import lax
from jax.experimental import pallas as pl
from jax.experimental.pallas import tpu as pltpu
from jax.sharding import PartitionSpec as P

HD = 128
MESH = pl.DeviceIdType.MESH
NEG_FILL = -1e30
COND_GAIN = 6.0
UNCOND_GAIN = -5.0
SCORE_GAIN = float(HD**-0.5 * np.log2(np.e))

Z_ORDER = (0, 1, 7, 2, 6, 3, 5, 4)
Z_COUNT = 8
SLOTS = 16
TOK = 96
HALF = 48
KV_ROWS = TOK + HALF
GROUPS = 4
PER_GROUP = 4
QUERIES = SLOTS * TOK
CHUNK = 4 * PER_GROUP * TOK
PART = QUERIES // 2

BF16 = jnp.bfloat16
F32 = jnp.float32


def row_partner(row, slot, sign):
    z, x = row // 2, row % 2
    dz = Z_ORDER[slot // 2]
    dz = dz if sign > 0 else (Z_COUNT - dz) % Z_COUNT
    return lax.rem(z + dz, Z_COUNT) * 2 + lax.rem(x + slot % 2, 2)


AROUND = tuple((dr, dc) for dr in (-1, 0, 1) for dc in (-1, 0, 1))
FRAMES, TROWS, TCOLS = 6, 4, 4
PLACES = TROWS * TCOLS
ROWS = FRAMES * PLACES
PADDED_ROWS = (FRAMES + 2) * PLACES


def pick_matrix():
    pick = np.zeros((3, 3, FRAMES // 2, TROWS, TCOLS, 9, FRAMES // 2, TROWS, TCOLS), np.float32)
    for e, g, f, i, j in np.ndindex(3, 3, FRAMES // 2, TROWS, TCOLS):
        r, c = i + e - 1, j + g - 1
        tile = AROUND.index((r // TROWS, c // TCOLS))
        pick[e, g, f, i, j, tile, f, r % TROWS, c % TCOLS] = 1.0
    return pick.reshape(9 * HALF, 9 * HALF)


def sigma_at(index):
    s = 1.0 - index / 50.0
    return 7.0 * s / (1.0 + 6.0 * s)


def attend(q_ref, o_ref, m_ref, part, key_ref, value_ref, usable):
    rows = pl.ds(pl.multiple_of(part * PART, PART), PART)
    scores = lax.dot_general(
        q_ref[rows, :], key_ref[...], (((1,), (1,)), ((), ())), preferred_element_type=F32
    )
    if usable is not None:
        scores = jnp.where(usable, scores, NEG_FILL)
    before = m_ref[rows, :]
    top = jnp.maximum(before, jnp.max(scores, axis=1, keepdims=True) * SCORE_GAIN)
    wide = jnp.concatenate([top] * (scores.shape[1] // HD), axis=1)
    weights = jnp.exp2(scores * SCORE_GAIN - wide).astype(BF16)
    o_ref[rows, :] = o_ref[rows, :] * jnp.exp2(before - top) + jnp.dot(
        weights, value_ref[...], preferred_element_type=F32
    )
    m_ref[rows, :] = top


def step_kernel(
    row_count, col_count,
    q_hbm, k_hbm, v_hbm, w_hbm, tk_hbm, tv_hbm, len_ref,
    lat_hbm, pick_hbm, step_ref, win_hbm, bin_hbm, wmid_hbm, bmid_hbm,
    guided_ref, out_ref,
    v_ref, w_ref, v_out, kv, q_ref, o_ref, m_ref, key_ref, value_ref, tk_ref, tv_ref, text_value, sh_out, sh_in,
    lat_in, pieces, lat_ref, pick_ref, win_ref, bin_ref, bmid_ref,
    mine, raw, raw_in, around, moved, shifted, w_in, wmid, act, center, ordered,
    k_send, k_recv, v_send, v_recv, q_send, q_recv, hop_send, hop_recv, sh_send, sh_recv,
    send, recv, w_sem, in_sem,
):
    branch, row, col = lax.axis_index("branch"), lax.axis_index("row"), lax.axis_index("col")
    y, core = col // 2, col % 2
    up = lax.rem(y + 1, 4) * 2 + core
    down = lax.rem(y + 3, 4) * 2 + core
    opposite = lax.rem(y + 2, 4) * 2 + core
    sibling = y * 2 + 1 - core

    def place(side, tile):
        dr, dc = AROUND[tile]
        return {
            "branch": lax.rem(branch + side, 2),
            "row": lax.rem(row + dr + row_count, row_count),
            "col": lax.rem(col + dc + col_count, col_count),
        }

    peers = [(side, tile) for side in (0, 1) for tile in range(9) if (side, tile) != (0, 4)]

    barrier = pltpu.get_barrier_semaphore()
    for slot in range(1, SLOTS):
        pl.semaphore_signal(
            barrier, inc=1, device_id={"row": row_partner(row, slot, 1)}, device_id_type=MESH
        )
    for other in (up, down, opposite, sibling):
        pl.semaphore_signal(barrier, inc=1, device_id={"col": other}, device_id_type=MESH)
    for side, tile in peers:
        pl.semaphore_signal(barrier, inc=1, device_id=place(side, tile), device_id_type=MESH)

    head_cols = pl.ds(pl.multiple_of(row * HD, HD), HD)
    loads = [
        pltpu.make_async_copy(src, dst, in_sem.at[i])
        for i, (src, dst) in enumerate(
            (
                (v_hbm.at[0], v_ref),
                (w_hbm, w_ref),
                (k_hbm.at[0, :, head_cols], kv.at[0, 0, pl.ds(0, TOK)]),
                (q_hbm.at[0, :, head_cols], q_ref.at[pl.ds(0, TOK)]),
                (tk_hbm.at[0, :, head_cols], tk_ref),
                (tv_hbm.at[0, :, head_cols], tv_ref),
                (win_hbm, win_ref),
                (bin_hbm, bin_ref),
                (bmid_hbm, bmid_ref),
                (pick_hbm, pick_ref),
                (lat_hbm, lat_in),
            )
        )
    ]
    for copy in loads:
        copy.start()

    def k_copy(slot):
        there = row_partner(row, slot, 1)
        return pltpu.make_async_remote_copy(
            src_ref=k_hbm.at[0, :, pl.ds(pl.multiple_of(there * HD, HD), HD)],
            dst_ref=kv.at[0, slot, pl.ds(0, TOK)],
            send_sem=k_send.at[slot],
            recv_sem=k_recv.at[slot],
            device_id={"row": there},
            device_id_type=MESH,
        )

    def v_copy(slot):
        there = row_partner(row, slot, 1)
        return pltpu.make_async_remote_copy(
            src_ref=v_out.at[there],
            dst_ref=kv.at[0, slot, pl.ds(TOK, HALF)],
            send_sem=v_send.at[slot],
            recv_sem=v_recv.at[slot],
            device_id={"row": there},
            device_id_type=MESH,
        )

    def q_copy(slot):
        there = row_partner(row, slot, 1)
        return pltpu.make_async_remote_copy(
            src_ref=q_hbm.at[0, :, pl.ds(pl.multiple_of(there * HD, HD), HD)],
            dst_ref=q_ref.at[pl.ds(slot * TOK, TOK)],
            send_sem=q_send.at[slot],
            recv_sem=q_recv.at[slot],
            device_id={"row": there},
            device_id_type=MESH,
        )

    def hop_copy(kind, group):
        src, dst, there = (
            (0, 1, up),
            (0, 2, down),
            (0, 3, opposite),
            (0, 4, sibling),
            (1, 5, sibling),
            (2, 6, sibling),
            (3, 7, sibling),
        )[kind]
        part = pl.ds(group * PER_GROUP, PER_GROUP)
        return pltpu.make_async_remote_copy(
            src_ref=kv.at[src, part],
            dst_ref=kv.at[dst, part],
            send_sem=hop_send.at[kind, group],
            recv_sem=hop_recv.at[kind, group],
            device_id={"col": there},
            device_id_type=MESH,
        )

    def share_copy(slot):
        return pltpu.make_async_remote_copy(
            src_ref=sh_out.at[slot],
            dst_ref=sh_in.at[slot],
            send_sem=sh_send.at[slot],
            recv_sem=sh_recv.at[slot],
            device_id={"row": row_partner(row, slot, -1)},
            device_id_type=MESH,
        )

    def copy_to(side, tile):
        if tile == 4:
            src, dst = raw, raw_in
        else:
            src, dst = mine, around.at[side, 8 - tile]
        return pltpu.make_async_remote_copy(
            src_ref=src,
            dst_ref=dst,
            send_sem=send.at[side, tile],
            recv_sem=recv.at[side, tile],
            device_id=place(side, tile),
            device_id_type=MESH,
        )

    near, far = range(1, 2 * PER_GROUP), range(2 * PER_GROUP, SLOTS)
    pl.semaphore_wait(barrier, SLOTS - 1 + 4 + len(peers))
    for slot in near:
        k_copy(slot).start()
    for slot in near:
        q_copy(slot).start()

    loads[0].wait()
    loads[1].wait()
    for head in range(SLOTS):
        cols = slice(head * HD, (head + 1) * HD)
        projected = lax.dot_general(
            v_ref[:, cols], w_ref[:, cols], (((1,), (1,)), ((), ())), preferred_element_type=F32
        )
        v_out[head] = jnp.concatenate([projected[0:HALF], projected[HALF:TOK]], axis=1).astype(BF16)
    for slot in near:
        v_copy(slot).start()
    for slot in far[:PER_GROUP]:
        k_copy(slot).start()
        v_copy(slot).start()
    for slot in far:
        q_copy(slot).start()
    for slot in far[PER_GROUP:]:
        k_copy(slot).start()
        v_copy(slot).start()
    kv[0, 0, TOK:KV_ROWS, :] = v_out[row]

    w_copies = []
    for b in range(3):
        for c in range(3):
            for a in range(3):
                w_copies.append(
                    pltpu.make_async_copy(
                        wmid_hbm.at[a, b, c],
                        wmid.at[b * 3 + c, pl.ds(a * 512, 512)],
                        w_sem.at[(b * 3 + c) * 3 + a],
                    )
                )
    for copy in w_copies:
        copy.start()

    o_ref[...] = jnp.zeros_like(o_ref)
    m_ref[...] = jnp.full_like(m_ref, NEG_FILL)
    kv_lane = lax.broadcasted_iota(jnp.int32, (HALF, HD), 1)
    ones = jnp.where(kv_lane == HD // 2, 1.0, 0.0).astype(F32)

    def first_hop(group):
        for slot in range(group * PER_GROUP, (group + 1) * PER_GROUP):
            if slot:
                k_copy(slot).wait_recv()
                v_copy(slot).wait_recv()
        for kind in (0, 1, 2, 3):
            hop_copy(kind, group).start()

    def second_hop(group):
        for kind in (0, 1, 2):
            hop_copy(kind, group).wait_recv()
        for kind in (4, 5, 6):
            hop_copy(kind, group).start()

    def from_sibling(group):
        for kind in (3, 4, 5, 6):
            hop_copy(kind, group).wait_recv()

    for copy in loads[2:]:
        copy.wait()
    first_hop(0)
    first_hop(1)

    cells = [
        (
            (f // 3) * 4 + p * 2 + s,
            pl.ds((f % 3) * PLACES + i * TCOLS, TCOLS),
            pl.ds(f * 64 + (2 * i + p) * 8 + s, TCOLS, stride=2),
        )
        for f in range(FRAMES)
        for i in range(TROWS)
        for p in range(2)
        for s in range(2)
    ]
    for piece, packed_rows, tile_rows in cells:
        pieces[piece, packed_rows, :] = lat_in[tile_rows, :]
    lat_ref[...] = jnp.concatenate([pieces[piece] for piece in range(8)], axis=1)

    zero = jnp.zeros((16, 512), BF16)
    for a in range(3):
        for r in range(4):
            for c in range(4):
                lanes = (((r // 2) * 2 + c // 2) * 4 + (r % 2) * 2 + c % 2) * 16
                for pp in range(2):
                    for ss in range(2):
                        inside = 0 <= r - pp < 3 and 0 <= c - ss < 3
                        w_in[
                            a * 256 + lanes : a * 256 + lanes + 16,
                            (pp * 2 + ss) * 512 : (pp * 2 + ss + 1) * 512,
                        ] = win_ref[a, r - pp, c - ss] if inside else zero

    text_rows = tk_ref.shape[0]
    text_projected = lax.dot_general(
        tv_ref[...], w_ref[:, head_cols], (((1,), (1,)), ((), ())), preferred_element_type=F32
    )
    text_lane = lax.broadcasted_iota(jnp.int32, (text_rows, HD // 2), 1)
    text_value[...] = jnp.concatenate(
        [text_projected, jnp.where(text_lane == 0, 1.0, 0.0).astype(F32)], axis=1
    ).astype(BF16)

    def attend_text(part):
        usable = lax.broadcasted_iota(jnp.int32, (PART, text_rows), 1) < len_ref[0]
        attend(q_ref, o_ref, m_ref, part, tk_ref, text_value, usable)

    def share_of(slot):
        out = o_ref[slot * TOK : (slot + 1) * TOK, :]
        share = out[:, 0 : HD // 2] / out[:, HD // 2 : HD // 2 + 1]
        return jnp.concatenate([share[0:HALF], share[HALF:TOK]], axis=1)

    def send_shares(slots):
        for slot in slots:
            sh_out[slot] = share_of(slot).astype(BF16)
            share_copy(slot).start()

    for slot in near:
        q_copy(slot).wait_recv()
    attend_text(0)
    second_hop(0)

    def before_1():
        from_sibling(0)

    def before_2():
        second_hop(1)
        first_hop(2)
        for slot in far:
            q_copy(slot).wait_recv()
        attend_text(1)

    def before_4():
        first_hop(3)

    def before_6():
        from_sibling(1)

    def before_7():
        second_hop(2)

    def before_8():
        second_hop(3)

    def before_10():
        from_sibling(2)

    def before_14():
        from_sibling(3)

    def before_15():
        send_shares(reversed(far))

    steps = {
        1: before_1,
        2: before_2,
        4: before_4,
        6: before_6,
        7: before_7,
        8: before_8,
        10: before_10,
        14: before_14,
        15: before_15,
    }

    @pl.loop(0, 4 * GROUPS)
    def _(unit):
        for when, step in steps.items():
            pl.when(unit == when)(step)
        opening = (19 - unit) // 16
        closing = (unit + 2) // 16
        even = 1 - unit % 2
        chunk = opening * (unit % 2) + (1 - opening) * (unit // 2)
        usual = (1 - closing) * (1 - even) + closing * even
        part = opening * (unit // 2) + (1 - opening) * usual
        fresh = opening * (1 - unit // 2) + (1 - opening) * even
        group, side, slab = chunk // 2, chunk % 2, chunk % 2

        @pl.when(fresh == 1)
        def _():
            for member in range(4):
                for slot in range(PER_GROUP):
                    at = (member * PER_GROUP + slot) * TOK
                    block = kv.at[4 * side + member, group * PER_GROUP + slot]
                    key_ref[slab, at : at + TOK, :] = block[0:TOK, :]
                    packed = block[TOK:KV_ROWS, :].astype(F32)
                    value_ref[slab, at : at + HALF, :] = jnp.where(
                        kv_lane < HD // 2, packed, ones
                    ).astype(BF16)
                    value_ref[slab, at + HALF : at + TOK, :] = jnp.where(
                        kv_lane < HD // 2, pltpu.roll(packed, HD // 2, 1), ones
                    ).astype(BF16)

        attend(q_ref, o_ref, m_ref, part, key_ref.at[slab], value_ref.at[slab], None)

    send_shares(reversed(near))
    velocity = share_of(0)
    for slot in range(1, SLOTS):
        share_copy(slot).wait_recv()
        velocity = velocity + sh_in[slot].astype(F32)

    index = step_ref[0].astype(F32)
    advance = sigma_at(index + 1.0) - sigma_at(index)
    first = branch == 0
    raw[...] = velocity
    keep = jnp.where(first, 1.0, 0.0)
    gain = jnp.where(first, COND_GAIN, UNCOND_GAIN) * advance
    mine[...] = lat_ref[...] * keep + velocity * gain
    for side, tile in peers:
        copy_to(side, tile).start()
    for side, tile in peers:
        copy_to(side, tile).wait_recv()

    cond = jnp.where(first, raw[...], raw_in[...])
    uncond = jnp.where(first, raw_in[...], raw[...])
    guided = COND_GAIN * cond + UNCOND_GAIN * uncond
    for piece in range(8):
        pieces[piece] = guided[:, piece * 16 : (piece + 1) * 16]
    for piece, packed_rows, tile_rows in cells:
        guided_ref[tile_rows, :] = pieces[piece, packed_rows, :]
    for tile, (dr, dc) in enumerate(AROUND):
        if tile == 4:
            value = lat_ref[...] + advance * guided
        else:
            there_row, there_col = row + dr, col + dc
            there = (
                (there_row >= 0)
                & (there_row < row_count)
                & (there_col >= 0)
                & (there_col < col_count)
            )
            value = (around[0, tile] + around[1, tile]) * jnp.where(there, 1.0, 0.0)
        moved[tile * HALF : (tile + 1) * HALF, :] = value.astype(BF16)

    picked = jnp.dot(pick_ref[...], moved[...], preferred_element_type=F32)
    lane = lax.broadcasted_iota(jnp.int32, (HALF, HD), 1)
    low = lane < HD // 2
    for e in range(3):
        for g in range(2):
            at = (e * 3 + g) * HALF
            here, right = picked[at : at + HALF], picked[at + HALF : at + 2 * HALF]
            early = jnp.where(low, here, pltpu.roll(right, HD // 2, 1)).astype(BF16)
            late = jnp.where(low, pltpu.roll(here, HD // 2, 1), right).astype(BF16)
            shifted[e, g, 0:PLACES, :] = early[0:PLACES]
            shifted[e, g, PLACES : 2 * PLACES, :] = early[0:PLACES]
            shifted[e, g, 2 * PLACES : 2 * PLACES + HALF, :] = early
            shifted[e, g, 2 * PLACES + HALF : PADDED_ROWS, :] = late

    patches = jnp.concatenate(
        [
            jnp.concatenate(
                [
                    shifted[db + du, dc, a * PLACES : a * PLACES + ROWS, :]
                    for a in range(3)
                    for du in range(2)
                ],
                axis=1,
            )
            for db in range(2)
            for dc in range(2)
        ],
        axis=0,
    )

    at = lax.broadcasted_iota(jnp.int32, (ROWS, 1), 0)
    row_at, col_at = (at // TCOLS) % TROWS, at % TCOLS
    bias_in = bin_ref[...]
    for pp in range(2):
        for ss in range(2):
            kind = pp * 2 + ss
            for half in range(2):
                cols = slice(half * 256, (half + 1) * 256)
                hidden = (
                    jnp.dot(
                        patches,
                        w_in[:, kind * 512 + half * 256 : kind * 512 + (half + 1) * 256],
                        preferred_element_type=F32,
                    )
                    + bias_in[:, cols]
                )
                for db in range(2):
                    for dc in range(2):
                        shift = db * 2 + dc
                        block = hidden[shift * ROWS : (shift + 1) * ROWS]
                        if (db, dc) == (1 - pp, 1 - ss):
                            center[kind, :, cols] = block
                        y_at = row * (2 * TROWS) - 1 + 2 * (row_at + db) + pp
                        x_at = col * (2 * TCOLS) - 1 + 2 * (col_at + dc) + ss
                        inside = (
                            (y_at >= 0)
                            & (y_at < row_count * 2 * TROWS)
                            & (x_at >= 0)
                            & (x_at < col_count * 2 * TCOLS)
                        )
                        value = jnp.where(inside, block * jax.nn.sigmoid(block), 0.0).astype(BF16)
                        act[kind, shift, 0:PLACES, cols] = value[0:PLACES]
                        act[kind, shift, PLACES : 2 * PLACES, cols] = value[0:PLACES]
                        act[kind, shift, 2 * PLACES : PADDED_ROWS, cols] = value

    total = None
    for b in range(3):
        for c in range(3):
            for a in range(3):
                w_copies[(b * 3 + c) * 3 + a].wait()
            window = []
            for pi in range(2):
                for si in range(2):
                    kind = ((pi + b) % 2) * 2 + (si + c) % 2
                    shift = ((pi + b) // 2) * 2 + (si + c) // 2
                    window.append(
                        jnp.concatenate(
                            [
                                act[kind, shift, a * PLACES : a * PLACES + ROWS, :]
                                for a in range(3)
                            ],
                            axis=1,
                        )
                    )
            term = jnp.dot(
                jnp.concatenate(window, axis=0), wmid[b * 3 + c], preferred_element_type=F32
            )
            total = term if total is None else total + term
    own = pl.ds(pl.multiple_of(branch * 256, 256), 256)
    for pi in range(2):
        for si in range(2):
            phase = pi * 2 + si
            result = (
                center[(1 - pi) * 2 + (1 - si), :, own]
                + total[phase * ROWS : (phase + 1) * ROWS]
                + bmid_ref[...]
            )
            for f in range(FRAMES):
                for i in range(TROWS):
                    at = f * PLACES + i * TCOLS
                    tile_rows = pl.ds(f * 64 + (2 * i + pi) * 8 + si, TCOLS, stride=2)
                    for side in range(2):
                        ordered[side, tile_rows, :] = result[
                            at : at + TCOLS, side * 128 : (side + 1) * 128
                        ]
    for side in range(2):
        out_ref[:, side * 128 : (side + 1) * 128] = ordered[side]

    for side, tile in peers:
        copy_to(side, tile).wait_send()
    for slot in range(1, SLOTS):
        k_copy(slot).wait_send()
        v_copy(slot).wait_send()
        q_copy(slot).wait_send()
        share_copy(slot).wait_send()
    for group in range(GROUPS):
        for kind in range(7):
            hop_copy(kind, group).wait_send()


def step(
    row_count, col_count,
    queries, keys, values, out_proj, text_keys, text_values, text_lengths,
    latent_cells, step_index, w_in, b_in, w_mid, b_mid,
):
    text_rows = text_keys.shape[1]
    vmem = pl.BlockSpec(memory_space=pltpu.VMEM)
    smem = pl.BlockSpec(memory_space=pltpu.SMEM)
    hbm = pl.BlockSpec(memory_space=pltpu.HBM)
    dma = pltpu.SemaphoreType.DMA
    return pl.pallas_call(
        functools.partial(step_kernel, row_count, col_count),
        out_shape=(
            jax.ShapeDtypeStruct((4 * ROWS, 16), F32),
            jax.ShapeDtypeStruct((4 * ROWS, 256), F32),
        ),
        in_specs=[hbm] * 6 + [smem] + [hbm] * 2 + [smem] + [hbm] * 4,
        out_specs=(vmem, vmem),
        scratch_shapes=[
            pltpu.VMEM((TOK, SLOTS * HD), BF16),
            pltpu.VMEM((HD // 2, SLOTS * HD), BF16),
            pltpu.VMEM((SLOTS, HALF, HD), BF16),
            pltpu.VMEM((8, SLOTS, KV_ROWS, HD), BF16),
            pltpu.VMEM((QUERIES, HD), BF16),
            pltpu.VMEM((QUERIES, HD), F32),
            pltpu.VMEM((QUERIES, HD), F32),
            pltpu.VMEM((2, CHUNK, HD), BF16),
            pltpu.VMEM((2, CHUNK, HD), BF16),
            pltpu.VMEM((text_rows, HD), BF16),
            pltpu.VMEM((text_rows, HD), BF16),
            pltpu.VMEM((text_rows, HD), BF16),
            pltpu.VMEM((SLOTS, HALF, HD), BF16),
            pltpu.VMEM((SLOTS, HALF, HD), BF16),
            pltpu.VMEM((4 * ROWS, 16), F32),
            pltpu.VMEM((8, HALF, 16), F32),
            pltpu.VMEM((HALF, HD), F32),
            pltpu.VMEM((9 * HALF, 9 * HALF), BF16),
            pltpu.VMEM((3, 3, 3, 16, 512), BF16),
            pltpu.VMEM((1, 512), F32),
            pltpu.VMEM((1, 256), F32),
            pltpu.VMEM((HALF, HD), F32),
            pltpu.VMEM((HALF, HD), F32),
            pltpu.VMEM((HALF, HD), F32),
            pltpu.VMEM((2, 9, HALF, HD), F32),
            pltpu.VMEM((9 * HALF, HD), BF16),
            pltpu.VMEM((3, 2, PADDED_ROWS, HD), BF16),
            pltpu.VMEM((768, 2048), BF16),
            pltpu.VMEM((9, 1536, 256), BF16),
            pltpu.VMEM((4, 4, PADDED_ROWS, 512), BF16),
            pltpu.VMEM((4, ROWS, 512), F32),
            pltpu.VMEM((2, 4 * ROWS, 128), F32),
            dma((SLOTS,)), dma((SLOTS,)), dma((SLOTS,)), dma((SLOTS,)), dma((SLOTS,)), dma((SLOTS,)),
            dma((7, GROUPS)), dma((7, GROUPS)), dma((SLOTS,)), dma((SLOTS,)),
            dma((2, 9)), dma((2, 9)), dma((27,)), dma((11,)),
        ],
        compiler_params=pltpu.CompilerParams(
            collective_id=0, has_side_effects=True, vmem_limit_bytes=58 * 2**20
        ),
        name="step",
    )(
        queries, keys, values, out_proj.T, text_keys, text_values, text_lengths,
        latent_cells, jnp.asarray(pick_matrix(), BF16), step_index,
        w_in, b_in[None, :], w_mid, b_mid[None, :],
    )


def local(
    row_count,
    col_count,
    queries,
    keys,
    values,
    text_keys,
    text_values,
    text_lengths,
    step_index,
    out_proj,
    latent,
    conv_in_w,
    conv_in_b,
    conv_mid_w,
    conv_mid_b,
):
    guided, decoded = step(
        row_count, col_count,
        queries, keys, values, out_proj, text_keys, text_values, text_lengths,
        latent.reshape(-1, 16), step_index, conv_in_w, conv_in_b, conv_mid_w, conv_mid_b,
    )
    return guided.reshape(latent.shape), decoded.reshape(latent.shape[:3] + (-1,))


def solution(mesh):
    return jax.shard_map(
        functools.partial(local, mesh.shape["row"], mesh.shape["col"]),
        mesh=mesh,
        in_specs=(
            P("branch", ("row", "col"), None),
            P("branch", ("row", "col"), None),
            P("branch", ("row", "col"), None),
            P("branch", None, None),
            P("branch", None, None),
            P("branch"),
            P(),
            P(),
            P(None, "row", "col", None),
            P(),
            P(),
            P(None, None, None, None, "branch"),
            P("branch"),
        ),
        out_specs=(P(None, "row", "col", None), P(None, "row", "col", "branch")),
        check_vma=False,
    )
```
